768 devices in a mesh: fsdp: 24 (over z_hi, x, core), table: 32 (over y, z_lo).
Axes of the slice: x: 4, y: 8, z: 12 (z_hi: 3, z_lo: 4; z = z_hi * 4 + z_lo), core: 2. Of those that a mesh axis runs over, the one named last changes fastest.
Arguments:
- looked_up: bfloat16 [1536, 512, 192], P('fsdp', 'table'), may hold values from -6 to 6
- assignment: int32 [512], replicated, may hold values from 0 to 511, each once
- flat_weights: bfloat16 [1044480], P('fsdp'), as said below
- cotangent: bfloat16 [1536, 256, 192], P(('fsdp', 'table')), may hold values from -6 to 6
Outputs:
- layer_out: bfloat16 [1536, 256, 192], P(('fsdp', 'table'))
- emb_grad: bfloat16 [1536, 512, 192], P('fsdp', 'table')
- weight_grad: float32 [1044480], P('fsdp')
The draws below stay inside these ranges and needn't reach their ends.
Inputs may be any that keep to these rules, and one draw needn't show every extreme that they name: `assignment`: every feature number appears exactly once. `flat_weights`: normal entries, each of the four weights scaled by its fan-in to the power -1/2 (512 for the first two, 4096 and 128 for the others).
All inputs are finite; a program needn't handle non-finite values.
Results may differ from the reference program's by a relative error of at most 0.0054.
Values may be sent and summed in bfloat16 or wider, within the bound.
A program may use at most 32 MiB of HBM per device.

```python
import jax
import jax.numpy as jnp
from jax import lax

NF = 512
D = 192
RANK = 8
HID = 128
NFM = 16
NLC = 240
NOUT = 256
GROUP_BATCH = 64
BATCH = 1536
PARAMS = 1044480
N_FSDP = 24


def draw_flat_weights(key, part):
    key = jax.random.fold_in(key, 7)
    value_entries = jax.random.normal(key, (PARAMS,), jnp.float32)
    position = jnp.arange(PARAMS)
    proj_end = NLC * NF + NF * RANK
    up_end = proj_end + NF * RANK * HID
    scaling = jnp.where(position < proj_end, NF ** (-0.5), jnp.where(position < up_end, (NF * RANK) ** (-0.5), HID ** (-0.5)))
    return (value_entries * scaling).astype(jnp.bfloat16)


def shard_levels(own_key, extent, cuts, least, high):
    gain, own = 1.0, jax.random.fold_in(own_key, 6)
    for axis_at, shards_of in cuts:
        steps = jnp.exp(jax.random.uniform(jax.random.fold_in(own, axis_at), (shards_of,), jnp.float32, least / len(cuts), high / len(cuts)))
        gain = gain * jnp.repeat(steps, extent[axis_at] // shards_of).reshape([-1 if axis == axis_at else 1 for axis in range(len(extent))])
    return gain


def noise(rng, extent, deviation, bound, cuts=(), held_as=jnp.bfloat16):
    entries = jax.random.normal(rng, extent, jnp.float32) * deviation
    if len(cuts) > 0:
        entries = shard_levels(rng, extent, cuts, -0.22, 0.18) * entries
    return jnp.clip(entries, min=-bound, max=bound).astype(held_as)


def setup_inputs(seed: int = 0) -> dict:
    keys = jax.random.split(jax.random.key(seed), 5)
    looked_up = noise(keys[0], (BATCH, NF, D), 1.0, 6.0, ((0, 24), (1, 32)))
    assignment = jax.random.permutation(keys[1], NF).astype(jnp.int32)
    flat_weights = draw_flat_weights(jax.random.fold_in(keys[4], 71), 0)
    cotangent = noise(keys[3], (BATCH, NOUT, D), 1.0, 6.0, ((0, 768),))
    return {"looked_up": looked_up, "assignment": assignment, "flat_weights": flat_weights, "cotangent": cotangent}


highest_precision = lax.Precision.HIGHEST

def ln_rows(value_entries):
    average = lax.optimization_barrier(jnp.mean(value_entries, axis=-1, keepdims=True))
    centred = value_entries - average
    spread = lax.optimization_barrier(jnp.mean(centred * centred, axis=-1, keepdims=True))
    inverse_std = lax.rsqrt(spread + 1e-05)
    return (centred * inverse_std, inverse_std)

def split_weights(flat_weights):
    lin_end = NLC * NF
    proj_end = lin_end + NF * RANK
    up_end = proj_end + NF * RANK * HID
    linear_weight_matrix = flat_weights[:lin_end].reshape(NLC, NF)
    proj_weight = flat_weights[lin_end:proj_end].reshape(NF, RANK)
    up_weight = flat_weights[proj_end:up_end].reshape(NF * RANK, HID)
    out_weight = flat_weights[up_end:].reshape(HID, NFM * D)
    return (linear_weight_matrix, proj_weight, up_weight, out_weight)

def layer_pass(input_rows, cotangent, linear_weight_matrix, proj_weight, up_weight, out_weight):
    samples = input_rows.shape[0]
    value_entries = input_rows.astype(jnp.float32)
    compressed = jnp.einsum('snd,nk->sdk', value_entries, proj_weight.astype(jnp.float32), precision=highest_precision).astype(jnp.bfloat16)
    pairwise = jnp.einsum('snd,sdk->snk', value_entries, compressed.astype(jnp.float32), precision=highest_precision)
    normed_full, pair_scale = ln_rows(pairwise.reshape(samples, NF * RANK))
    normed = normed_full.astype(jnp.bfloat16)
    preact = jnp.dot(normed, up_weight, preferred_element_type=jnp.float32)
    hidden = jax.nn.silu(preact).astype(jnp.bfloat16)
    mixed = jnp.dot(hidden, out_weight, preferred_element_type=jnp.float32).reshape(samples, NFM, D)
    linear_output = jnp.einsum('rg,pgm->prm', linear_weight_matrix.astype(jnp.float32), value_entries, precision=highest_precision)
    joined = jnp.concatenate([mixed, linear_output], axis=1)
    out_normed, out_scale = ln_rows(joined)
    result = out_normed.astype(jnp.bfloat16)
    upstream = cotangent.astype(jnp.float32)
    d_joined = out_scale * (upstream - lax.optimization_barrier(jnp.mean(upstream, axis=-1, keepdims=True)) - out_normed * lax.optimization_barrier(jnp.mean(upstream * out_normed, axis=-1, keepdims=True)))
    d_low = d_joined.astype(jnp.bfloat16)
    d_mixed = d_low[:, :NFM].reshape(samples, NFM * D)
    linear_branch_gradient = d_low[:, NFM:]
    grad_out = jnp.dot(hidden.T, d_mixed, preferred_element_type=jnp.float32)
    d_hidden = jnp.dot(d_mixed, out_weight.T, preferred_element_type=jnp.float32)
    logistic = jax.nn.sigmoid(preact)
    d_preact = (d_hidden * logistic * (1.0 + preact * (1.0 - logistic))).astype(jnp.bfloat16)
    grad_up = jnp.dot(normed.T, d_preact, preferred_element_type=jnp.float32)
    d_normed = jnp.dot(d_preact, up_weight.T, preferred_element_type=jnp.float32)
    d_flat = pair_scale * (d_normed - lax.optimization_barrier(jnp.mean(d_normed, axis=-1, keepdims=True)) - normed_full * lax.optimization_barrier(jnp.mean(d_normed * normed_full, axis=-1, keepdims=True)))
    d_pairwise = d_flat.reshape(samples, NF, RANK).astype(jnp.bfloat16)
    pair_f = d_pairwise.astype(jnp.float32)
    from_pairs = jnp.einsum('snk,sdk->snd', pair_f, compressed.astype(jnp.float32), precision=highest_precision)
    d_compressed = jnp.einsum('snd,snk->sdk', value_entries, pair_f, precision=highest_precision).astype(jnp.bfloat16)
    comp_f = d_compressed.astype(jnp.float32)
    from_proj = jnp.einsum('sdk,nk->snd', comp_f, proj_weight.astype(jnp.float32), precision=highest_precision)
    grad_proj = jnp.einsum('snd,sdk->nk', value_entries, comp_f, precision=highest_precision)
    linear_features = linear_branch_gradient.astype(jnp.float32)
    linear_weight_gradient = jnp.einsum('ayi,axi->yx', linear_features, value_entries, precision=highest_precision)
    linear_branch_result = jnp.einsum('uj,cuy->cjy', linear_weight_matrix.astype(jnp.float32), linear_features, precision=highest_precision)
    d_input = (from_pairs + from_proj + linear_branch_result).astype(jnp.bfloat16)
    gradients = jnp.concatenate([linear_weight_gradient.reshape(-1), grad_proj.reshape(-1), grad_up.reshape(-1), grad_out.reshape(-1)])
    return (result, d_input, gradients)

def reference(looked_up, assignment, flat_weights, cotangent):
    linear_weight_matrix, proj_weight, up_weight, out_weight = split_weights(flat_weights)
    inverse = jnp.argsort(assignment).astype(jnp.int32)
    ordered = jnp.take(looked_up, inverse, axis=1).reshape(N_FSDP, GROUP_BATCH, NF, D)
    upstream = cotangent.reshape(N_FSDP, GROUP_BATCH, NOUT, D)

    def one_group(running, blocks):
        result, d_input, gradients = layer_pass(blocks[0], blocks[1], linear_weight_matrix, proj_weight, up_weight, out_weight)
        return (running + gradients, (result, d_input))
    totals, stacked = lax.scan(one_group, jnp.zeros((PARAMS,), jnp.float32), (ordered, upstream))
    layer_out = stacked[0].reshape(BATCH, NOUT, D)
    d_model = stacked[1].reshape(BATCH, NF, D)
    emb_grad = jnp.take(d_model, assignment.astype(jnp.int32), axis=1)
    weight_grad = totals / jnp.float32(BATCH)
    return (layer_out, emb_grad, weight_grad)
```

```python
import functools

import jax
import jax.numpy as jnp
import numpy as np
from jax import lax
from jax.experimental import pallas as pl
from jax.experimental.pallas import tpu as pltpu
from jax.sharding import PartitionSpec as P

NF = 512
D = 192
RANK = 8
HID = 128
NFM = 16
NLC = 240
NT = 32
NFS = 24
SHARD_ROWS = 340
PIECE_ROWS = 352
HALF_ROWS = PIECE_ROWS // 2
PROJ_ROW = 960
UP_ROW = 992
OUT_ROW = 5088
TOTAL_ROWS = 8160
SAMPLES = 1536.0
SLOTS = 16
MESH = pl.DeviceIdType.MESH
f32 = jnp.float32
bf16 = jnp.bfloat16


def _tables():
    owned = [[] for _ in range(NT)]
    for t in range(NT):
        for m in range(16):
            for k in range(8):
                owned[t].append((UP_ROW + 8 * (32 * m + t) + k, m * 8 + k))
        if t < 24:
            for h in range(HID):
                owned[t].append((OUT_ROW + 24 * h + t, 128 + h))
        for q in range(4):
            for m in range(8):
                if 32 * m + t < NLC:
                    owned[t].append((4 * (32 * m + t) + q, 256 + q * 8 + m))
        if t >= 3:
            owned[t].append((PROJ_ROW + t - 3, 288))
        if 3 <= t <= 5:
            owned[t].append((PROJ_ROW + 26 + t, 289))
    to_block = np.full((NT, 384), -1, np.int32)
    to_row = np.full((NFS, NT * SLOTS), -1, np.int32)
    seen = 0
    for t in range(NT):
        filled = [0] * NFS
        for row, place in sorted(owned[t]):
            f = row // SHARD_ROWS
            slot = filled[f]
            filled[f] += 1
            assert slot < SLOTS
            to_block[t, place] = f * SLOTS + slot
            to_row[f, t * SLOTS + slot] = row - f * SHARD_ROWS
            seen += 1
    assert seen == TOTAL_ROWS
    return to_block, to_row


TO_BLOCK, TO_ROW = _tables()


def iota(shape, dim):
    return lax.broadcasted_iota(jnp.int32, shape, dim)


def one_hot(condition):
    return jnp.where(condition, 1.0, 0.0).astype(bf16)


def nn(a, b):
    return lax.dot_general(a, b, (((1,), (0,)), ((), ())), preferred_element_type=f32)


def nt(a, b):
    return lax.dot_general(a, b, (((1,), (1,)), ((), ())), preferred_element_type=f32)


def tn(a, b):
    return lax.dot_general(a, b, (((0,), (0,)), ((), ())), preferred_element_type=f32)


def lanes(x, start, size):
    return lax.slice_in_dim(x, start, start + size, axis=1)


def rows(x, start, size):
    return lax.slice_in_dim(x, start, start + size, axis=0)


def arrive_kernel(lk_ref, w_ref, arr_ref, all_ref, pack, a_send, a_recv, w_send, w_recv, own_sem):
    t = lax.axis_index("table")
    f = lax.axis_index("fsdp")
    z, x, c = f // 8, (f // 2) % 4, f % 2

    def fs(zz, xx, cc):
        return ((z + zz) % 3) * 8 + ((x + xx) % 4) * 2 + (c + cc) % 2

    barrier = pltpu.get_barrier_semaphore()

    def greet(s, carry):
        pl.semaphore_signal(barrier, inc=1, device_id={"table": (t + s) % NT}, device_id_type=MESH)
        return carry

    near = (fs(1, 0, 0), fs(2, 0, 0), fs(0, 1, 0), fs(0, 3, 0), fs(0, 0, 1))
    for other in near:
        pl.semaphore_signal(barrier, inc=1, device_id={"fsdp": other}, device_id_type=MESH)
    lax.fori_loop(1, NT, greet, 0)

    pack[:, :, 0:D] = lk_ref[:, 0]
    pack[:, :, D : 2 * D] = lk_ref[:, 1]
    pl.semaphore_wait(barrier, NT - 1 + len(near))

    def piece(src, shard, index, to, part=None):
        dst = all_ref.at[shard]
        if part is not None:
            src = src.at[pl.ds(part * HALF_ROWS, HALF_ROWS)]
            dst = dst.at[pl.ds(part * HALF_ROWS, HALF_ROWS)]
        return pltpu.make_async_remote_copy(
            src_ref=src,
            dst_ref=dst,
            send_sem=w_send.at[index],
            recv_sem=w_recv.at[index],
            device_id={"fsdp": to},
            device_id_type=MESH,
        )

    sent = []

    def send(*args):
        copy = piece(*args)
        copy.start()
        sent.append(copy)

    def forward(shard, index, to, part=None):
        send(all_ref.at[shard], shard, index, to, part)

    def arrived(shard, index, part=None):
        piece(all_ref.at[shard], shard, index, f, part).wait_recv()

    up, down, right, left, sibling = near
    send(w_ref, f, 0, up)
    send(w_ref, f, 1, down)
    send(w_ref, f, 2, right)
    send(w_ref, f, 5, left)
    send(w_ref, f, 14, sibling)
    own = pltpu.make_async_copy(w_ref, all_ref.at[f], own_sem.at[0])
    own.start()
    mine = pltpu.make_async_copy(pack.at[t], arr_ref.at[t], own_sem.at[1])
    mine.start()

    def row_copy(s):
        to = (t + s) % NT
        return pltpu.make_async_remote_copy(
            src_ref=pack.at[to],
            dst_ref=arr_ref.at[t],
            send_sem=a_send.at[s],
            recv_sem=a_recv.at[s],
            device_id={"table": to},
            device_id_type=MESH,
        )

    def start_rows(s, carry):
        row_copy(s).start()
        return carry

    lax.fori_loop(1, NT, start_rows, 0)

    for index, dz in ((0, 2), (1, 1)):
        shard = fs(dz, 0, 0)
        arrived(shard, index)
        forward(shard, 2 + dz, right)
        forward(shard, 5 + dz, left)
        forward(shard, 14 + dz, sibling)
    for dz in (0, 2, 1):
        shard = fs(dz, 3, 0)
        arrived(shard, 2 + dz)
        forward(shard, 8 + dz, right, 0)
        forward(shard, 17 + dz, sibling)
        shard = fs(dz, 1, 0)
        arrived(shard, 5 + dz)
        forward(shard, 11 + dz, left, 1)
        forward(shard, 20 + dz, sibling)
    for dz in (0, 2, 1):
        shard = fs(dz, 2, 0)
        arrived(shard, 8 + dz, 0)
        forward(shard, 23 + dz, sibling, 0)
        arrived(shard, 11 + dz, 1)
        forward(shard, 26 + dz, sibling, 1)
    for dz in (0, 2, 1):
        arrived(fs(dz, 0, 1), 14 + dz)
        arrived(fs(dz, 3, 1), 17 + dz)
        arrived(fs(dz, 1, 1), 20 + dz)
        arrived(fs(dz, 2, 1), 23 + dz, 0)
        arrived(fs(dz, 2, 1), 26 + dz, 1)

    def wait_rows(s, carry):
        row_copy(s).wait_recv()
        return carry

    lax.fori_loop(1, NT, wait_rows, 0)
    own.wait()
    mine.wait()
    for copy in sent:
        copy.wait_send()

    def wait_sent(s, carry):
        row_copy(s).wait_send()
        return carry

    lax.fori_loop(1, NT, wait_sent, 0)


def spread(values, row_mod):
    lane = iota((16, 128), 1)
    keep = lane % 8 == row_mod
    out = []
    for v in range(32):
        source = lanes(values, 128 * (v // 8), 128)
        taken = jnp.take_along_axis(source, 16 * (v % 8) + lane // 8, axis=1)
        out.append(jnp.where(keep, taken, 0.0))
    return out


def gather_back(wide, row_mod):
    lane = iota((16, 128), 1)
    index = 8 * (lane % 16) + row_mod
    out = []
    for u in range(4):
        total = jnp.zeros((16, 128), f32)
        for w in range(8):
            taken = jnp.take_along_axis(lanes(wide, 128 * (8 * u + w), 128), index, axis=1)
            total = jnp.where(lane // 16 == w, taken, total)
        out.append(total)
    return jnp.concatenate(out, axis=1)


def layer_kernel(arr_ref, all_ref, as_row_ref, as_col_ref, cot_ref, out_ref, back_ref, msg_ref, nat, wout, msg):
    for f in range(NFS):
        nat[pl.ds(SHARD_ROWS * f, SHARD_ROWS), :] = all_ref[f].astype(f32)[:SHARD_ROWS]
    lin = jnp.concatenate([nat[pl.ds(q, NLC, stride=4), :] for q in range(4)], axis=1)
    lin = jnp.concatenate([lin, jnp.zeros((16, NF), f32)], axis=0).astype(bf16)
    for chunk in range(24):
        wout[:, 128 * chunk : 128 * chunk + 128] = nat[pl.ds(OUT_ROW + chunk, HID, stride=24), :].astype(bf16)
    proj_rows = nat[PROJ_ROW : PROJ_ROW + 32, :].astype(bf16)
    up = nat[UP_ROW : UP_ROW + NF * RANK, :].astype(bf16)

    r8 = one_hot(iota((8, 128), 1) % 8 == iota((8, 128), 0))
    flat_mask = iota((NF, 128), 1) // 8 == iota((NF, 128), 0) % 16
    picked = nn(one_hot(iota((NF, 32), 1) == iota((NF, 32), 0) // 16), proj_rows)
    picked = jnp.where(flat_mask, picked, 0.0).astype(bf16)
    proj_t = nt(r8, picked).astype(bf16)

    arrived = arr_ref[...]
    by_model = one_hot(as_row_ref[...] == iota((NF, NF), 0))
    by_table = one_hot(as_col_ref[...] == iota((NF, NF), 1))
    x = nn(by_model, arrived).astype(bf16)
    eye = one_hot(iota((2 * D, 2 * D), 0) == iota((2 * D, 2 * D), 1))
    xt = nt(eye, x).astype(bf16)

    half = iota((16, 2 * D), 1) // D == iota((16, 2 * D), 0) // 8
    comp = nn(proj_t, x)
    comp = jnp.concatenate([comp, comp], axis=0)
    comp = jnp.where(half, comp, 0.0).astype(bf16)
    pair = nt(comp, x)

    def per_sample(v):
        total = jnp.sum(v.reshape(2, 8, NF), axis=(1, 2), keepdims=True) * (1.0 / (NF * RANK))
        return jnp.broadcast_to(total, (2, 8, NF)).reshape(16, NF)

    centred = pair - per_sample(pair)
    pair_scale = lax.rsqrt(per_sample(centred * centred) + 1e-05)
    normed_full = centred * pair_scale
    normed = normed_full.astype(bf16)
    row_mod = iota((16, 128), 0) % 8
    wide = jnp.concatenate(spread(normed.astype(f32), row_mod), axis=1).astype(bf16)
    preact = jnp.sum(nn(wide, up).reshape(2, 8, HID), axis=1)
    logistic = 1.0 / (1.0 + jnp.exp(-preact))
    hidden = (preact / (1.0 + jnp.exp(-preact))).astype(bf16)
    mixed = nn(hidden, wout[...])

    def by_pairs(b):
        return jnp.concatenate([lanes(mixed[b : b + 1], 384 * e, 384) for e in range(8)], axis=0)

    m0, m1 = by_pairs(0), by_pairs(1)
    mix = jnp.concatenate(
        [
            jnp.concatenate([lanes(m0, 0, D), lanes(m1, 0, D)], axis=1),
            jnp.concatenate([lanes(m0, D, D), lanes(m1, D, D)], axis=1),
        ],
        axis=0,
    )
    mix = jnp.concatenate([jnp.zeros((112, 2 * D), f32), mix], axis=0).T
    linear = nt(xt, lin)
    joined = jnp.concatenate([lanes(linear, 0, 128), lanes(linear, 128, 128) + mix], axis=1)

    lane = iota((256, 256), 1)
    here = jnp.where(lane < NLC, lane + NFM, 2 * ((lane - NLC) % 8) + (lane - NLC) // 8)
    order = one_hot(here == iota((256, 256), 0))
    upstream = nn(cot_ref[...], order).reshape(2, D, 256)

    joined = joined.reshape(2, D, 256)
    mean = lambda v: jnp.mean(v, axis=1, keepdims=True)
    centred_out = joined - mean(joined)
    out_scale = lax.rsqrt(mean(centred_out * centred_out) + 1e-05)
    out_normed = centred_out * out_scale
    out_ref[...] = nt(out_normed.reshape(2 * D, 256).astype(bf16), order).astype(bf16)
    d_low = out_scale * (upstream - mean(upstream) - out_normed * mean(upstream * out_normed))
    d_low = d_low.reshape(2 * D, 256).astype(bf16)

    at = iota((272, 256), 0)
    wanted = 32 * (at % 8) + at // 8
    wanted = jnp.where(at >= 256, at - 256 + NLC, jnp.where(wanted < NLC, wanted, -1))
    d_rows = nt(one_hot(wanted == iota((272, 256), 1)), d_low)
    d_mix = rows(d_rows, 256, 16)
    grad_lin = nt(rows(d_rows, 0, 256).astype(bf16), x)
    d_pairs = [
        jnp.concatenate([lanes(d_mix[0:8], b * D, D), lanes(d_mix[8:16], b * D, D)], axis=1) for b in range(2)
    ]
    d_mixed = jnp.concatenate(
        [jnp.concatenate([d_pairs[b][e : e + 1] for e in range(8)], axis=1) for b in range(2)], axis=0
    )
    d_hidden = nt(d_mixed.astype(bf16), wout[...])
    d_preact = (d_hidden * logistic * (1.0 + preact * (1.0 - logistic))).astype(bf16)

    copies = jnp.concatenate(
        [jnp.broadcast_to(d_preact.astype(f32)[b : b + 1], (8, HID)) for b in range(2)], axis=0
    ).astype(bf16)
    d_normed = gather_back(nt(copies, up), row_mod)
    d_pair = pair_scale * (d_normed - per_sample(d_normed) - normed_full * per_sample(d_normed * normed_full))
    d_pair = d_pair.astype(bf16)

    d_comp = jnp.where(half, nn(d_pair, x), 0.0)
    d_comp = (d_comp[0:8] + d_comp[8:16]).astype(bf16)
    left = jnp.concatenate([comp, d_comp.astype(f32).astype(bf16)], axis=0)
    right = jnp.concatenate([d_pair, proj_t], axis=0)
    d_input = (tn(left, right) + nn(d_low, lin)).astype(bf16)
    back_ref[...] = nt(by_table, d_input).astype(bf16).reshape(NT, 16, 2 * D)

    grad_proj = nt(d_comp, x).astype(bf16)
    flat = jnp.where(flat_mask, tn(grad_proj, r8), 0.0).astype(bf16)
    at = iota((64, NF), 0)
    wanted = jnp.where(
        at < 32, jnp.where(at >= 3, at - 3, -1), jnp.where((at >= 35) & (at <= 37), at - 6, -1)
    )
    proj_out = nn(one_hot(wanted == iota((64, NF), 1) // 16), flat)
    p_lane = iota((NF, NF), 1)
    to_owner = one_hot(iota((NF, NF), 0) == (p_lane % 16) * 32 + p_lane // 16)
    by_owner = spread(nn(normed, to_owner), row_mod)
    msg[:, :, 256:384] = jnp.zeros((NT, 16, 128), f32)
    msg[:, 0:8, 0:256] = lanes(grad_lin, 0, 256).reshape(NT, 8, 256)
    msg[:, 8:16, 0:256] = lanes(grad_lin, 256, 256).reshape(NT, 8, 256)
    msg[:, 2:4, 256:384] = jnp.broadcast_to(hidden.astype(f32)[None], (NT, 2, HID))
    msg[:, 8:10, 256:384] = jnp.broadcast_to(d_preact.astype(f32)[None], (NT, 2, HID))
    for t in range(NT):
        msg[t, 0:2, 256:384] = jnp.sum(by_owner[t].reshape(2, 8, 128), axis=1)
        msg[t, 4:5, 256:384] = proj_out[t : t + 1]
        msg[t, 5:6, 256:384] = proj_out[32 + t : 33 + t]
        if t < 24:
            msg[t, 10:12, 256:384] = lanes(d_mixed, 128 * t, 128)
    msg_ref[...] = msg[...].astype(bf16)


def leave_kernel(
    back_ref, msg_ref, block_ref, row_ref, emb_ref, grad_ref,
    rec, got, blocks, parts, mine, whole, b_send, b_recv, m_send, m_recv, f_send, f_recv, g_send, g_recv,
):
    t = lax.axis_index("table")
    f = lax.axis_index("fsdp")

    barrier = pltpu.get_barrier_semaphore()

    def greet_table(s, carry):
        pl.semaphore_signal(barrier, inc=1, device_id={"table": (t + s) % NT}, device_id_type=MESH)
        return carry

    def greet_fsdp(s, carry):
        pl.semaphore_signal(barrier, inc=1, device_id={"fsdp": (f + s) % NFS}, device_id_type=MESH)
        return carry

    lax.fori_loop(1, NT, greet_table, 0)
    lax.fori_loop(1, NFS, greet_fsdp, 0)
    pl.semaphore_wait(barrier, NT - 1 + NFS - 1)

    def to_table(s, src, dst, send_sem, recv_sem):
        to = (t + s) % NT
        return pltpu.make_async_remote_copy(
            src_ref=src if src is mine else src.at[to],
            dst_ref=dst.at[t],
            send_sem=send_sem.at[s],
            recv_sem=recv_sem.at[s],
            device_id={"table": to},
            device_id_type=MESH,
        )

    def to_fsdp(s):
        to = (f + s) % NFS
        return pltpu.make_async_remote_copy(
            src_ref=blocks.at[to],
            dst_ref=parts.at[f],
            send_sem=f_send.at[s],
            recv_sem=f_recv.at[s],
            device_id={"fsdp": to},
            device_id_type=MESH,
        )

    def each(n, act):
        def step(s, carry):
            act(s)
            return carry

        lax.fori_loop(1, n, step, 0)

    msg_copy = lambda s: to_table(s, msg_ref, got, m_send, m_recv)
    row_copy = lambda s: to_table(s, back_ref, rec, b_send, b_recv)
    all_copy = lambda s: to_table(s, mine, whole, g_send, g_recv)

    each(NT, lambda s: msg_copy(s).start())
    each(NT, lambda s: row_copy(s).start())
    got[pl.ds(t, 1)] = msg_ref[pl.ds(t, 1)]
    rec[pl.ds(t, 1)] = back_ref[pl.ds(t, 1)]
    place = one_hot(iota((NFS * SLOTS, 384), 0) == block_ref[pl.ds(t, 1), :])
    final = one_hot(iota((PIECE_ROWS, NT * SLOTS), 0) == row_ref[pl.ds(f, 1), :])

    each(NT, lambda s: msg_copy(s).wait_recv())
    linear = jnp.sum(got[:, :, 0:256].astype(f32), axis=0)
    factors = got[:, :, 256:384].astype(f32)
    first = factors[:, 0:8].reshape(NT * 8, 128)
    second = factors[:, 8:16].reshape(NT * 8, 128).astype(bf16)
    at = iota((NT * 8, 128), 0) % 8
    left = jnp.concatenate([jnp.where(at < 2, first, 0.0), jnp.where((at == 2) | (at == 3), first, 0.0)], axis=1)
    products = tn(left.astype(bf16), second)
    tail = jnp.sum(factors[:, 0:8], axis=0)[4:6]
    sums = jnp.concatenate(
        [
            products,
            linear[0:8, 0:128],
            linear[0:8, 128:256],
            linear[8:16, 0:128],
            linear[8:16, 128:256],
            tail,
            jnp.zeros((94, 128), f32),
        ],
        axis=0,
    ).astype(bf16)
    blocks[...] = nn(place, sums).astype(bf16).reshape(NFS, SLOTS, 128)

    each(NFS, lambda s: to_fsdp(s).start())
    parts[pl.ds(f, 1)] = blocks[pl.ds(f, 1)]
    each(NFS, lambda s: to_fsdp(s).wait_recv())
    mine[...] = jnp.sum(parts[...].astype(f32), axis=0).astype(bf16)

    each(NT, lambda s: all_copy(s).start())
    whole[pl.ds(t, 1)] = mine[...][None]
    each(NT, lambda s: all_copy(s).wait_recv())
    grad_ref[...] = nn(final, whole[...].reshape(NT * SLOTS, 128)) * (1.0 / SAMPLES)

    each(NT, lambda s: row_copy(s).wait_recv())
    emb_ref[:, 0] = rec[:, :, 0:D]
    emb_ref[:, 1] = rec[:, :, D : 2 * D]
    each(NT, lambda s: msg_copy(s).wait_send())
    each(NT, lambda s: row_copy(s).wait_send())
    each(NT, lambda s: all_copy(s).wait_send())
    each(NFS, lambda s: to_fsdp(s).wait_send())


VMEM = pl.BlockSpec(memory_space=pltpu.VMEM)
LIMIT = 56 * 1024 * 1024


def arrive(looked, shard):
    return pl.pallas_call(
        arrive_kernel,
        out_shape=(
            jax.ShapeDtypeStruct((NT, 16, 2 * D), bf16),
            jax.ShapeDtypeStruct((NFS, PIECE_ROWS, 128), bf16),
        ),
        in_specs=[VMEM] * 2,
        out_specs=(VMEM, VMEM),
        scratch_shapes=[
            pltpu.VMEM((NT, 16, 2 * D), bf16),
            pltpu.SemaphoreType.DMA((NT,)),
            pltpu.SemaphoreType.DMA((NT,)),
            pltpu.SemaphoreType.DMA((29,)),
            pltpu.SemaphoreType.DMA((29,)),
            pltpu.SemaphoreType.DMA((2,)),
        ],
        compiler_params=pltpu.CompilerParams(collective_id=0, has_side_effects=True, vmem_limit_bytes=LIMIT),
    )(looked, shard)


def layer(arrived, weights, as_row, as_col, cotangent):
    return pl.pallas_call(
        layer_kernel,
        out_shape=(
            jax.ShapeDtypeStruct((2 * D, 256), bf16),
            jax.ShapeDtypeStruct((NT, 16, 2 * D), bf16),
            jax.ShapeDtypeStruct((NT, 16, 2 * D), bf16),
        ),
        in_specs=[VMEM] * 5,
        out_specs=(VMEM, VMEM, VMEM),
        scratch_shapes=[
            pltpu.VMEM((TOTAL_ROWS, 128), f32),
            pltpu.VMEM((HID, NFM * D), bf16),
            pltpu.VMEM((NT, 16, 2 * D), f32),
        ],
        compiler_params=pltpu.CompilerParams(vmem_limit_bytes=LIMIT),
    )(arrived, weights, as_row, as_col, cotangent)


def leave(back, message):
    return pl.pallas_call(
        leave_kernel,
        out_shape=(
            jax.ShapeDtypeStruct((NT, 2, 16, D), bf16),
            jax.ShapeDtypeStruct((PIECE_ROWS, 128), f32),
        ),
        in_specs=[VMEM] * 4,
        out_specs=(VMEM, VMEM),
        scratch_shapes=[
            pltpu.VMEM((NT, 16, 2 * D), bf16),
            pltpu.VMEM((NT, 16, 2 * D), bf16),
            pltpu.VMEM((NFS, SLOTS, 128), bf16),
            pltpu.VMEM((NFS, SLOTS, 128), bf16),
            pltpu.VMEM((SLOTS, 128), bf16),
            pltpu.VMEM((NT, SLOTS, 128), bf16),
        ]
        + [pltpu.SemaphoreType.DMA((NT,))] * 8,
        compiler_params=pltpu.CompilerParams(collective_id=1, has_side_effects=True, vmem_limit_bytes=LIMIT),
    )(back, message, jnp.asarray(TO_BLOCK), jnp.asarray(TO_ROW))


def shards(looked_up, assignment, flat_weights, cotangent):
    shard = jnp.pad(flat_weights.reshape(SHARD_ROWS, 128), ((0, PIECE_ROWS - SHARD_ROWS), (0, 0)))
    arrived, weights = arrive(looked_up.reshape(NT, 2, 16, D), shard)
    out, back, message = layer(
        arrived.reshape(NF, 2 * D),
        weights,
        assignment.reshape(1, NF),
        assignment.reshape(NF, 1),
        cotangent.transpose(0, 2, 1).reshape(2 * D, 256),
    )
    emb, grad = leave(back, message)
    layer_out = out.reshape(2, D, 256).transpose(0, 2, 1)
    return layer_out, emb.reshape(2 * NT, 16, D), grad[:SHARD_ROWS].reshape(SHARD_ROWS * 128)


def solution(mesh):
    return jax.shard_map(
        shards,
        mesh=mesh,
        in_specs=(P("fsdp", "table", None), P(), P("fsdp"), P(("fsdp", "table"), None, None)),
        out_specs=(P(("fsdp", "table"), None, None), P("fsdp", "table", None), P("fsdp")),
        check_vma=False,
    )
```

```python
import functools

import jax
import jax.numpy as jnp
import numpy as np
from jax import lax
from jax.experimental import pallas as pl
from jax.experimental.pallas import tpu as pltpu
from jax.sharding import PartitionSpec as P

NF = 512
D = 192
RANK = 8
HID = 128
NFM = 16
NLC = 240
NT = 32
NFS = 24
SHARD_ROWS = 340
PIECE_ROWS = 352
HALF_ROWS = PIECE_ROWS // 2
PROJ_ROW = 960
UP_ROW = 992
OUT_ROW = 5088
TOTAL_ROWS = 8160
SAMPLES = 1536.0
SLOTS = 16
MESH = pl.DeviceIdType.MESH
f32 = jnp.float32
bf16 = jnp.bfloat16


def _tables():
    owned = [[] for _ in range(NT)]
    for t in range(NT):
        for m in range(16):
            for k in range(8):
                owned[t].append((UP_ROW + 8 * (32 * m + t) + k, m * 8 + k))
        if t < 24:
            for h in range(HID):
                owned[t].append((OUT_ROW + 24 * h + t, 128 + h))
        for q in range(4):
            for m in range(8):
                if 32 * m + t < NLC:
                    owned[t].append((4 * (32 * m + t) + q, 256 + q * 8 + m))
        if t >= 3:
            owned[t].append((PROJ_ROW + t - 3, 288))
        if 3 <= t <= 5:
            owned[t].append((PROJ_ROW + 26 + t, 289))
    to_block = np.full((NT, 384), -1, np.int32)
    to_row = np.full((NFS, NT * SLOTS), -1, np.int32)
    seen = 0
    for t in range(NT):
        filled = [0] * NFS
        for row, place in sorted(owned[t]):
            f = row // SHARD_ROWS
            slot = filled[f]
            filled[f] += 1
            assert slot < SLOTS
            to_block[t, place] = f * SLOTS + slot
            to_row[f, t * SLOTS + slot] = row - f * SHARD_ROWS
            seen += 1
    assert seen == TOTAL_ROWS
    return to_block, to_row


TO_BLOCK, TO_ROW = _tables()


def iota(shape, dim):
    return lax.broadcasted_iota(jnp.int32, shape, dim)


def one_hot(condition):
    return jnp.where(condition, 1.0, 0.0).astype(bf16)


def nn(a, b):
    return lax.dot_general(a, b, (((1,), (0,)), ((), ())), preferred_element_type=f32)


def nt(a, b):
    return lax.dot_general(a, b, (((1,), (1,)), ((), ())), preferred_element_type=f32)


def tn(a, b):
    return lax.dot_general(a, b, (((0,), (0,)), ((), ())), preferred_element_type=f32)


def lanes(x, start, size):
    return lax.slice_in_dim(x, start, start + size, axis=1)


def rows(x, start, size):
    return lax.slice_in_dim(x, start, start + size, axis=0)


def spread(values, row_mod):
    lane = iota((16, 128), 1)
    keep = lane % 8 == row_mod
    out = []
    for v in range(32):
        source = lanes(values, 128 * (v // 8), 128)
        taken = jnp.take_along_axis(source, 16 * (v % 8) + lane // 8, axis=1)
        out.append(jnp.where(keep, taken, 0.0))
    return out


def gather_back(wide, row_mod):
    lane = iota((16, 128), 1)
    index = 8 * (lane % 16) + row_mod
    out = []
    for u in range(4):
        total = jnp.zeros((16, 128), f32)
        for w in range(8):
            taken = jnp.take_along_axis(lanes(wide, 128 * (8 * u + w), 128), index, axis=1)
            total = jnp.where(lane // 16 == w, taken, total)
        out.append(total)
    return jnp.concatenate(out, axis=1)


def whole_kernel(
    lk_ref, w_ref, as_row_ref, cot_ref, block_ref, out_ref, rec_ref, whole_ref,
    pack, padded, arr, all_ref, nat, wout, by_model, order, upstream, lin_msg, fac_msg, back, fac,
    got_lin, got_fac, blocks, parts, mine,
    own_sem, a_send, a_recv, w_send, w_recv, l_send, l_recv, m_send, m_recv, b_send, b_recv, f_send, f_recv, g_send, g_recv,
):
    t = lax.axis_index("table")
    f = lax.axis_index("fsdp")
    z, xx, c = f // 8, (f // 2) % 4, f % 2

    def fs(dz, dx, dc):
        return ((z + dz) % 3) * 8 + ((xx + dx) % 4) * 2 + (c + dc) % 2

    def each(n, act):
        def step(s, carry):
            act(s)
            return carry

        lax.fori_loop(1, n, step, 0)

    def to_table(src, dst, send_sem, recv_sem):
        def copy(s):
            to = (t + s) % NT
            return pltpu.make_async_remote_copy(
                src_ref=src if src is mine else src.at[to],
                dst_ref=dst.at[t],
                send_sem=send_sem.at[s],
                recv_sem=recv_sem.at[s],
                device_id={"table": to},
                device_id_type=MESH,
            )

        return copy

    def to_fsdp(s):
        to = (f + s) % NFS
        return pltpu.make_async_remote_copy(
            src_ref=blocks.at[to],
            dst_ref=parts.at[f],
            send_sem=f_send.at[s],
            recv_sem=f_recv.at[s],
            device_id={"fsdp": to},
            device_id_type=MESH,
        )

    row_in = to_table(pack, arr, a_send, a_recv)
    lin_out = to_table(lin_msg, got_lin, l_send, l_recv)
    fac_out = to_table(fac_msg, got_fac, m_send, m_recv)
    row_out = to_table(back, rec_ref, b_send, b_recv)
    all_out = to_table(mine, whole_ref, g_send, g_recv)

    barrier = pltpu.get_barrier_semaphore()
    near = (fs(1, 0, 0), fs(2, 0, 0), fs(0, 1, 0), fs(0, 3, 0), fs(0, 0, 1))
    each(NT, lambda s: pl.semaphore_signal(barrier, inc=1, device_id={"table": (t + s) % NT}, device_id_type=MESH))
    for other in near:
        pl.semaphore_signal(barrier, inc=1, device_id={"fsdp": other}, device_id_type=MESH)
    padded[0:SHARD_ROWS] = w_ref[...]
    padded[SHARD_ROWS:PIECE_ROWS] = jnp.zeros((PIECE_ROWS - SHARD_ROWS, 128), bf16)
    pack[:, :, 0:D] = lk_ref[:, 0]
    pack[:, :, D : 2 * D] = lk_ref[:, 1]
    pl.semaphore_wait(barrier, NT - 1 + len(near))

    def piece(src, shard, index, to, part=None):
        dst = all_ref.at[shard]
        if part is not None:
            src = src.at[pl.ds(part * HALF_ROWS, HALF_ROWS)]
            dst = dst.at[pl.ds(part * HALF_ROWS, HALF_ROWS)]
        return pltpu.make_async_remote_copy(
            src_ref=src,
            dst_ref=dst,
            send_sem=w_send.at[index],
            recv_sem=w_recv.at[index],
            device_id={"fsdp": to},
            device_id_type=MESH,
        )

    sent = []

    def send(*args):
        copy = piece(*args)
        copy.start()
        sent.append(copy)

    def forward(shard, index, to, part=None):
        send(all_ref.at[shard], shard, index, to, part)

    def arrived(shard, index, part=None):
        piece(all_ref.at[shard], shard, index, f, part).wait_recv()

    up_z, down_z, right, left, sibling = near
    send(padded, f, 0, up_z)
    send(padded, f, 1, down_z)
    send(padded, f, 2, right)
    send(padded, f, 5, left)
    send(padded, f, 14, sibling)
    each(NT, lambda s: row_in(s).start())
    all_ref[pl.ds(f, 1)] = padded[...][None]
    arr[pl.ds(t, 1)] = pack[pl.ds(t, 1)]

    by_model[...] = one_hot(as_row_ref[...] == iota((NF, NF), 0))
    lane = iota((256, 256), 1)
    here = jnp.where(lane < NLC, lane + NFM, 2 * ((lane - NLC) % 8) + (lane - NLC) // 8)
    order[...] = one_hot(here == iota((256, 256), 0))
    upstream[...] = nn(cot_ref[...], order[...])

    def turn(dz):
        shard = fs(dz, 3, 0)
        arrived(shard, 2 + dz)
        forward(shard, 8 + dz, right, 0)
        forward(shard, 17 + dz, sibling)
        shard = fs(dz, 1, 0)
        arrived(shard, 5 + dz)
        forward(shard, 11 + dz, left, 1)
        forward(shard, 20 + dz, sibling)

    def opposite(dz):
        shard = fs(dz, 2, 0)
        arrived(shard, 8 + dz, 0)
        forward(shard, 23 + dz, sibling, 0)
        arrived(shard, 11 + dz, 1)
        forward(shard, 26 + dz, sibling, 1)

    def assemble(dz, dx):
        column = ((z + dz) % 3) * 4 + (xx + dx) % 4
        both = [all_ref[2 * column + core].astype(f32)[:SHARD_ROWS] for core in range(2)]
        at = pl.multiple_of(2 * SHARD_ROWS * column, 8)
        nat[pl.ds(at, 2 * SHARD_ROWS), :] = jnp.concatenate(both, axis=0)

    def others(dz):
        arrived(fs(dz, 0, 1), 14 + dz)
        assemble(dz, 0)
        arrived(fs(dz, 3, 1), 17 + dz)
        assemble(dz, 3)
        arrived(fs(dz, 1, 1), 20 + dz)
        assemble(dz, 1)
        arrived(fs(dz, 2, 1), 23 + dz, 0)
        arrived(fs(dz, 2, 1), 26 + dz, 1)
        assemble(dz, 2)

    turn(0)
    for index, dz in ((0, 2), (1, 1)):
        shard = fs(dz, 0, 0)
        arrived(shard, index)
        forward(shard, 2 + dz, right)
        forward(shard, 5 + dz, left)
        forward(shard, 14 + dz, sibling)
    opposite(0)
    turn(2)
    turn(1)
    others(0)
    opposite(2)
    opposite(1)

    each(NT, lambda s: row_in(s).wait_recv())
    x = nn(by_model[...], arr[...].reshape(NF, 2 * D)).astype(bf16)
    eye = one_hot(iota((2 * D, 2 * D), 0) == iota((2 * D, 2 * D), 1))
    xt = nt(eye, x).astype(bf16)

    others(2)
    others(1)

    lin = jnp.concatenate([nat[pl.ds(q, NLC, stride=4), :] for q in range(4)], axis=1)
    lin = jnp.concatenate([lin, jnp.zeros((16, NF), f32)], axis=0).astype(bf16)
    for chunk in range(24):
        wout[:, 128 * chunk : 128 * chunk + 128] = nat[pl.ds(OUT_ROW + chunk, HID, stride=24), :].astype(bf16)
    proj_rows = nat[PROJ_ROW : PROJ_ROW + 32, :].astype(bf16)
    up = nat[UP_ROW : UP_ROW + NF * RANK, :].astype(bf16)

    r8 = one_hot(iota((8, 128), 1) % 8 == iota((8, 128), 0))
    flat_mask = iota((NF, 128), 1) // 8 == iota((NF, 128), 0) % 16
    picked = nn(one_hot(iota((NF, 32), 1) == iota((NF, 32), 0) // 16), proj_rows)
    picked = jnp.where(flat_mask, picked, 0.0).astype(bf16)
    proj_t = nt(r8, picked).astype(bf16)

    half = iota((16, 2 * D), 1) // D == iota((16, 2 * D), 0) // 8
    comp = nn(proj_t, x)
    comp = jnp.concatenate([comp, comp], axis=0)
    comp = jnp.where(half, comp, 0.0).astype(bf16)
    pair = nt(comp, x)

    def per_sample(v):
        total = jnp.sum(v.reshape(2, 8, NF), axis=(1, 2), keepdims=True) * (1.0 / (NF * RANK))
        return jnp.broadcast_to(total, (2, 8, NF)).reshape(16, NF)

    centred = pair - per_sample(pair)
    pair_scale = lax.rsqrt(per_sample(centred * centred) + 1e-05)
    normed_full = centred * pair_scale
    normed = normed_full.astype(bf16)
    row_mod = iota((16, 128), 0) % 8
    wide = jnp.concatenate(spread(normed.astype(f32), row_mod), axis=1).astype(bf16)
    preact = jnp.sum(nn(wide, up).reshape(2, 8, HID), axis=1)
    logistic = 1.0 / (1.0 + jnp.exp(-preact))
    hidden = (preact / (1.0 + jnp.exp(-preact))).astype(bf16)
    mixed = nn(hidden, wout[...])

    def by_pairs(b):
        return jnp.concatenate([lanes(mixed[b : b + 1], 384 * e, 384) for e in range(8)], axis=0)

    m0, m1 = by_pairs(0), by_pairs(1)
    mix = jnp.concatenate(
        [
            jnp.concatenate([lanes(m0, 0, D), lanes(m1, 0, D)], axis=1),
            jnp.concatenate([lanes(m0, D, D), lanes(m1, D, D)], axis=1),
        ],
        axis=0,
    )
    mix = jnp.concatenate([jnp.zeros((112, 2 * D), f32), mix], axis=0).T
    linear = nt(xt, lin)
    joined = jnp.concatenate([lanes(linear, 0, 128), lanes(linear, 128, 128) + mix], axis=1)

    joined = joined.reshape(2, D, 256)
    mean = lambda v: jnp.mean(v, axis=1, keepdims=True)
    centred_out = joined - mean(joined)
    out_scale = lax.rsqrt(mean(centred_out * centred_out) + 1e-05)
    out_normed = centred_out * out_scale
    cot = upstream[...].reshape(2, D, 256)
    d_low = out_scale * (cot - mean(cot) - out_normed * mean(cot * out_normed))
    d_low = d_low.reshape(2 * D, 256).astype(bf16)

    at = iota((272, 256), 0)
    wanted = 32 * (at % 8) + at // 8
    wanted = jnp.where(at >= 256, at - 256 + NLC, jnp.where(wanted < NLC, wanted, -1))
    d_rows = nt(one_hot(wanted == iota((272, 256), 1)), d_low)
    grad_lin = nt(rows(d_rows, 0, 256).astype(bf16), x)
    lin_msg[...] = jnp.concatenate(
        [lanes(grad_lin, 0, 256).reshape(NT, 8, 256), lanes(grad_lin, 256, 256).reshape(NT, 8, 256)], axis=1
    ).astype(bf16)
    each(NT, lambda s: lin_out(s).start())

    d_mix = rows(d_rows, 256, 16)
    d_pairs = [
        jnp.concatenate([lanes(d_mix[0:8], b * D, D), lanes(d_mix[8:16], b * D, D)], axis=1) for b in range(2)
    ]
    d_mixed = jnp.concatenate(
        [jnp.concatenate([d_pairs[b][e : e + 1] for e in range(8)], axis=1) for b in range(2)], axis=0
    )
    d_hidden = nt(d_mixed.astype(bf16), wout[...])
    d_preact = (d_hidden * logistic * (1.0 + preact * (1.0 - logistic))).astype(bf16)

    copies = jnp.concatenate(
        [jnp.broadcast_to(d_preact.astype(f32)[b : b + 1], (8, HID)) for b in range(2)], axis=0
    ).astype(bf16)
    d_normed = gather_back(nt(copies, up), row_mod)
    d_pair = pair_scale * (d_normed - per_sample(d_normed) - normed_full * per_sample(d_normed * normed_full))
    d_pair = d_pair.astype(bf16)

    d_comp = jnp.where(half, nn(d_pair, x), 0.0)
    d_comp = (d_comp[0:8] + d_comp[8:16]).astype(bf16)

    grad_proj = nt(d_comp, x).astype(bf16)
    flat = jnp.where(flat_mask, tn(grad_proj, r8), 0.0).astype(bf16)
    at = iota((64, NF), 0)
    wanted = jnp.where(
        at < 32, jnp.where(at >= 3, at - 3, -1), jnp.where((at >= 35) & (at <= 37), at - 6, -1)
    )
    proj_out = nn(one_hot(wanted == iota((64, NF), 1) // 16), flat)
    p_lane = iota((NF, NF), 1)
    to_owner = one_hot(iota((NF, NF), 0) == (p_lane % 16) * 32 + p_lane // 16)
    by_owner = spread(nn(normed, to_owner), row_mod)
    fac[...] = jnp.zeros((NT, 16, 128), f32)
    fac[:, 2:4] = jnp.broadcast_to(hidden.astype(f32)[None], (NT, 2, HID))
    fac[:, 8:10] = jnp.broadcast_to(d_preact.astype(f32)[None], (NT, 2, HID))
    for i in range(NT):
        fac[i, 0:2] = jnp.sum(by_owner[i].reshape(2, 8, 128), axis=1)
        fac[i, 4:5] = proj_out[i : i + 1]
        fac[i, 5:6] = proj_out[32 + i : 33 + i]
        if i < 24:
            fac[i, 10:12] = lanes(d_mixed, 128 * i, 128)
    fac_msg[...] = fac[...].astype(bf16)
    each(NT, lambda s: fac_out(s).start())

    left_side = jnp.concatenate([comp, d_comp], axis=0)
    right_side = jnp.concatenate([d_pair, proj_t], axis=0)
    d_input = (tn(left_side, right_side) + nn(d_low, lin)).astype(bf16)
    back[...] = lax.dot_general(
        by_model[...], d_input, (((0,), (1,)), ((), ())), preferred_element_type=f32
    ).astype(bf16).reshape(NT, 16, 2 * D)
    each(NT, lambda s: row_out(s).start())

    got_lin[pl.ds(t, 1)] = lin_msg[pl.ds(t, 1)]
    got_fac[pl.ds(t, 1)] = fac_msg[pl.ds(t, 1)]
    rec_ref[pl.ds(t, 1)] = back[pl.ds(t, 1)]
    out_ref[...] = nt(out_normed.reshape(2 * D, 256).astype(bf16), order[...]).astype(bf16)
    place = one_hot(iota((NFS * SLOTS, 384), 0) == block_ref[pl.ds(t, 1), :])

    each(NT, lambda s: lin_out(s).wait_recv())
    linear = jnp.sum(got_lin[...].astype(f32), axis=0)
    each(NT, lambda s: fac_out(s).wait_recv())
    factors = got_fac[...].astype(f32)
    first = factors[:, 0:8].reshape(NT * 8, 128)
    second = factors[:, 8:16].reshape(NT * 8, 128).astype(bf16)
    at = iota((NT * 8, 128), 0) % 8
    left_side = jnp.concatenate([jnp.where(at < 2, first, 0.0), jnp.where((at == 2) | (at == 3), first, 0.0)], axis=1)
    products = tn(left_side.astype(bf16), second)
    tail = jnp.sum(factors[:, 0:8], axis=0)[4:6]
    sums = jnp.concatenate(
        [
            products,
            linear[0:8, 0:128],
            linear[0:8, 128:256],
            linear[8:16, 0:128],
            linear[8:16, 128:256],
            tail,
            jnp.zeros((94, 128), f32),
        ],
        axis=0,
    ).astype(bf16)
    blocks[...] = nn(place, sums).astype(bf16).reshape(NFS, SLOTS, 128)

    each(NFS, lambda s: to_fsdp(s).start())
    parts[pl.ds(f, 1)] = blocks[pl.ds(f, 1)]
    each(NFS, lambda s: to_fsdp(s).wait_recv())
    mine[...] = jnp.sum(parts[...].astype(f32), axis=0).astype(bf16)

    each(NT, lambda s: all_out(s).start())
    whole_ref[pl.ds(t, 1)] = mine[...][None]
    each(NT, lambda s: all_out(s).wait_recv())
    each(NT, lambda s: row_out(s).wait_recv())

    for copy in sent:
        copy.wait_send()
    for copies in (row_in, lin_out, fac_out, row_out, all_out):
        each(NT, lambda s: copies(s).wait_send())
    each(NFS, lambda s: to_fsdp(s).wait_send())


def finish_kernel(out_ref, rec_ref, whole_ref, row_ref, layer_ref, emb_ref, grad_ref):
    f = lax.axis_index("fsdp")
    layer_ref[...] = out_ref[...]
    emb_ref[:, 0] = rec_ref[:, :, 0:D]
    emb_ref[:, 1] = rec_ref[:, :, D : 2 * D]
    final = one_hot(iota((SHARD_ROWS, NT * SLOTS), 0) == row_ref[pl.ds(f, 1), :])
    grad_ref[...] = nn(final, whole_ref[...].reshape(NT * SLOTS, 128)) * (1.0 / SAMPLES)


VMEM = pl.BlockSpec(memory_space=pltpu.VMEM)
LIMIT = 40 * 1024 * 1024


def shape(dtype, *size):
    return jax.ShapeDtypeStruct(size, dtype)


def whole(looked, shard, as_row, cotangent):
    return pl.pallas_call(
        whole_kernel,
        out_shape=(shape(bf16, 2 * D, 256), shape(bf16, NT, 16, 2 * D), shape(bf16, NT, SLOTS, 128)),
        in_specs=[VMEM] * 5,
        out_specs=(VMEM,) * 3,
        scratch_shapes=[
            pltpu.VMEM((NT, 16, 2 * D), bf16),
            pltpu.VMEM((PIECE_ROWS, 128), bf16),
            pltpu.VMEM((NT, 16, 2 * D), bf16),
            pltpu.VMEM((NFS, PIECE_ROWS, 128), bf16),
            pltpu.VMEM((TOTAL_ROWS, 128), f32),
            pltpu.VMEM((HID, NFM * D), bf16),
            pltpu.VMEM((NF, NF), bf16),
            pltpu.VMEM((256, 256), bf16),
            pltpu.VMEM((2 * D, 256), f32),
            pltpu.VMEM((NT, 16, 256), bf16),
            pltpu.VMEM((NT, 16, 128), bf16),
            pltpu.VMEM((NT, 16, 2 * D), bf16),
            pltpu.VMEM((NT, 16, 128), f32),
            pltpu.VMEM((NT, 16, 256), bf16),
            pltpu.VMEM((NT, 16, 128), bf16),
            pltpu.VMEM((NFS, SLOTS, 128), bf16),
            pltpu.VMEM((NFS, SLOTS, 128), bf16),
            pltpu.VMEM((SLOTS, 128), bf16),
            pltpu.SemaphoreType.DMA((2,)),
        ]
        + [pltpu.SemaphoreType.DMA((NT,))] * 14,
        compiler_params=pltpu.CompilerParams(collective_id=0, has_side_effects=True, vmem_limit_bytes=LIMIT),
    )(looked, shard, as_row, cotangent, jnp.asarray(TO_BLOCK))


def finish(out, rec, gathered):
    return pl.pallas_call(
        finish_kernel,
        out_shape=(shape(bf16, 2 * D, 256), shape(bf16, NT, 2, 16, D), shape(f32, SHARD_ROWS, 128)),
        in_specs=[VMEM] * 4,
        out_specs=(VMEM,) * 3,
    )(out, rec, gathered, jnp.asarray(TO_ROW))


def shards(looked_up, assignment, flat_weights, cotangent):
    out, rec, gathered = whole(
        looked_up.reshape(NT, 2, 16, D),
        flat_weights.reshape(SHARD_ROWS, 128),
        assignment.reshape(1, NF),
        cotangent.transpose(0, 2, 1).reshape(2 * D, 256),
    )
    layer_out, emb, grad = finish(out, rec, gathered)
    return layer_out.reshape(2, D, 256).transpose(0, 2, 1), emb.reshape(2 * NT, 16, D), grad.reshape(SHARD_ROWS * 128)


def solution(mesh):
    return jax.shard_map(
        shards,
        mesh=mesh,
        in_specs=(P("fsdp", "table", None), P(), P("fsdp"), P(("fsdp", "table"), None, None)),
        out_specs=(P(("fsdp", "table"), None, None), P("fsdp", "table", None), P("fsdp")),
        check_vma=False,
    )
```

```python
import functools

import jax
import jax.numpy as jnp
import numpy as np
from jax import lax
from jax.experimental import pallas as pl
from jax.experimental.pallas import tpu as pltpu
from jax.sharding import PartitionSpec as P

NF = 512
D = 192
RANK = 8
HID = 128
NFM = 16
NLC = 240
NT = 32
NFS = 24
SHARD_ROWS = 340
PIECE_ROWS = 352
HALF_ROWS = PIECE_ROWS // 2
PROJ_ROW = 960
UP_ROW = 992
OUT_ROW = 5088
TOTAL_ROWS = 8160
SAMPLES = 1536.0
SLOTS = 16
MESH = pl.DeviceIdType.MESH
f32 = jnp.float32
bf16 = jnp.bfloat16


def _tables():
    owned = [[] for _ in range(NT)]
    for t in range(NT):
        for m in range(16):
            for k in range(8):
                owned[t].append((UP_ROW + 8 * (32 * m + t) + k, m * 8 + k))
        if t < 24:
            for h in range(HID):
                owned[t].append((OUT_ROW + 24 * h + t, 128 + h))
        for q in range(4):
            for m in range(8):
                if 32 * m + t < NLC:
                    owned[t].append((4 * (32 * m + t) + q, 256 + q * 8 + m))
        if t >= 3:
            owned[t].append((PROJ_ROW + t - 3, 288))
        if 3 <= t <= 5:
            owned[t].append((PROJ_ROW + 26 + t, 289))
    to_block = np.full((NT, 384), -1, np.int32)
    to_row = np.full((NFS, NT * SLOTS), -1, np.int32)
    seen = 0
    for t in range(NT):
        filled = [0] * NFS
        for row, place in sorted(owned[t]):
            f = row // SHARD_ROWS
            slot = filled[f]
            filled[f] += 1
            assert slot < SLOTS
            to_block[t, place] = f * SLOTS + slot
            to_row[f, t * SLOTS + slot] = row - f * SHARD_ROWS
            seen += 1
    assert seen == TOTAL_ROWS
    return to_block, to_row


TO_BLOCK, TO_ROW = _tables()


def iota(shape, dim):
    return lax.broadcasted_iota(jnp.int32, shape, dim)


def one_hot(condition):
    return jnp.where(condition, 1.0, 0.0).astype(bf16)


def nn(a, b):
    return lax.dot_general(a, b, (((1,), (0,)), ((), ())), preferred_element_type=f32)


def nt(a, b):
    return lax.dot_general(a, b, (((1,), (1,)), ((), ())), preferred_element_type=f32)


def tn(a, b):
    return lax.dot_general(a, b, (((0,), (0,)), ((), ())), preferred_element_type=f32)


def lanes(x, start, size):
    return lax.slice_in_dim(x, start, start + size, axis=1)


def rows(x, start, size):
    return lax.slice_in_dim(x, start, start + size, axis=0)


def spread(values, row_mod):
    lane = iota((16, 128), 1)
    keep = lane % 8 == row_mod
    out = []
    for v in range(32):
        source = lanes(values, 128 * (v // 8), 128)
        taken = jnp.take_along_axis(source, 16 * (v % 8) + lane // 8, axis=1)
        out.append(jnp.where(keep, taken, 0.0))
    return out


def gather_back(wide, row_mod):
    lane = iota((16, 128), 1)
    index = 8 * (lane % 16) + row_mod
    out = []
    for u in range(4):
        total = jnp.zeros((16, 128), f32)
        for w in range(8):
            taken = jnp.take_along_axis(lanes(wide, 128 * (8 * u + w), 128), index, axis=1)
            total = jnp.where(lane // 16 == w, taken, total)
        out.append(total)
    return jnp.concatenate(out, axis=1)


def whole_kernel(
    lk_hbm, w_hbm, as_row_hbm, cot_hbm, block_hbm, out_hbm, rec_ref, whole_ref,
    lk_ref, w_ref, as_row_ref, cot_ref, block_ref, out_ref, pack, padded, arr, all_ref, nat, wout, by_model, order, upstream, pair_out, pair_in, kept, lin_msg, fac_msg, back,
    got_lin, got_fac, blocks, parts, mine,
    own_sem, in_sem, w_send, w_recv, ex_send, ex_recv,
):
    t = lax.axis_index("table")
    f = lax.axis_index("fsdp")
    z, xx, c = f // 8, (f // 2) % 4, f % 2

    def fs(dz, dx, dc):
        return ((z + dz) % 3) * 8 + ((xx + dx) % 4) * 2 + (c + dc) % 2

    def each(n, act):
        def step(s, carry):
            act(s)
            return carry

        lax.fori_loop(1, n, step, 0)

    class Exchange:
        def __init__(self, axis, src, dst, index):
            me, self.n = (t, NT) if axis == "table" else (f, NFS)

            def copy(s):
                to = (me + s) % self.n
                return pltpu.make_async_remote_copy(
                    src_ref=src if src is mine else src.at[to],
                    dst_ref=dst.at[me],
                    send_sem=ex_send.at[index],
                    recv_sem=ex_recv.at[index],
                    device_id={axis: to},
                    device_id_type=MESH,
                )

            self.copy = copy
            every = dst.at[pl.ds(0, self.n - 1)]
            self.every = lambda: pltpu.make_async_remote_copy(
                src_ref=every,
                dst_ref=every,
                send_sem=ex_send.at[index],
                recv_sem=ex_recv.at[index],
                device_id={axis: me},
                device_id_type=MESH,
            )

        def start(self):
            each(self.n, lambda s: self.copy(s).start())
            started.append(self)

        def wait(self):
            self.every().wait_recv()
            received.append(self)

        def wait_send(self):
            self.every().wait_send()

    started = []
    received = []
    row_in = Exchange("table", pack, arr, 0)
    lin_out = Exchange("table", lin_msg, got_lin, 1)
    fac_out = Exchange("table", fac_msg, got_fac, 2)
    row_out = Exchange("table", back, rec_ref, 3)
    all_out = Exchange("table", mine, whole_ref, 4)
    to_fsdp = Exchange("fsdp", blocks, parts, 5)

    def local(src, dst, index):
        return pltpu.make_async_copy(src, dst, in_sem.at[index])

    inputs = [
        local(w_hbm, w_ref, 0),
        local(lk_hbm, lk_ref, 1),
        local(as_row_hbm, as_row_ref, 2),
        local(cot_hbm, cot_ref, 3),
        local(block_hbm, block_ref, 4),
    ]
    for copy in inputs:
        copy.start()

    barrier = pltpu.get_barrier_semaphore()
    near = (fs(1, 0, 0), fs(2, 0, 0), fs(0, 1, 0), fs(0, 3, 0), fs(0, 0, 1))
    each(NT, lambda s: pl.semaphore_signal(barrier, inc=1, device_id={"table": (t + s) % NT}, device_id_type=MESH))
    for other in near:
        pl.semaphore_signal(barrier, inc=1, device_id={"fsdp": other}, device_id_type=MESH)
    inputs[0].wait()
    padded[0:SHARD_ROWS] = w_ref[...]
    padded[SHARD_ROWS:PIECE_ROWS] = jnp.zeros((PIECE_ROWS - SHARD_ROWS, 128), bf16)
    inputs[1].wait()
    pack[:, :, 0:D] = lk_ref[:, 0]
    pack[:, :, D : 2 * D] = lk_ref[:, 1]
    pl.semaphore_wait(barrier, NT - 1 + len(near))

    def piece(src, shard, part, index, to):
        at = pl.ds(part * HALF_ROWS, HALF_ROWS)
        return pltpu.make_async_remote_copy(
            src_ref=src.at[at],
            dst_ref=all_ref.at[shard, at],
            send_sem=w_send.at[index],
            recv_sem=w_recv.at[index],
            device_id={"fsdp": to},
            device_id_type=MESH,
        )

    sent = []
    locals_started = []

    def drain():
        for copy in locals_started:
            copy.wait()
        for copy in sent:
            copy.wait_send()
        for exchange in started:
            if exchange not in received:
                exchange.wait()
        for exchange in started:
            exchange.wait_send()

    def send(*args):
        copy = piece(*args)
        copy.start()
        sent.append(copy)

    def forward(shard, part, index, to):
        send(all_ref.at[shard], shard, part, index + part, to)

    def arrived(shard, part, index):
        piece(all_ref.at[shard], shard, part, index + part, f).wait_recv()

    up_z, down_z, right, left, sibling = near
    for part in range(2):
        send(padded, f, part, part, up_z)
        send(padded, f, part, 2 + part, down_z)
    for part in range(2):
        send(padded, f, part, 4 + part, right)
        send(padded, f, part, 10 + part, left)
        send(padded, f, part, 22 + part, sibling)
    row_in.start()
    all_ref[pl.ds(f, 1)] = padded[...][None]
    arr[pl.ds(t, 1)] = pack[pl.ds(t, 1)]

    for copy in inputs[2:]:
        copy.wait()
    by_model[...] = one_hot(as_row_ref[...] == iota((NF, NF), 0))
    lane = iota((256, 256), 1)
    here = jnp.where(lane < NLC, lane + NFM, 2 * ((lane - NLC) % 8) + (lane - NLC) // 8)
    order[...] = one_hot(here == iota((256, 256), 0))
    upstream[...] = nn(cot_ref[...], order[...])

    def from_z(part):
        for index, dz in ((0, 2), (2, 1)):
            shard = fs(dz, 0, 0)
            arrived(shard, part, index)
            forward(shard, part, 4 + 2 * dz, right)
            forward(shard, part, 10 + 2 * dz, left)
            forward(shard, part, 22 + 8 * dz, sibling)

    def turn(dz, part):
        shard = fs(dz, 3, 0)
        arrived(shard, part, 4 + 2 * dz)
        if part == 0:
            forward(shard, part, 16 + 2 * dz, right)
        forward(shard, part, 22 + 8 * dz + 6, sibling)
        shard = fs(dz, 1, 0)
        arrived(shard, part, 10 + 2 * dz)
        if part == 1:
            forward(shard, part, 16 + 2 * dz, left)
        forward(shard, part, 22 + 8 * dz + 2, sibling)

    def opposite(dz, part):
        shard = fs(dz, 2, 0)
        arrived(shard, part, 16 + 2 * dz)
        forward(shard, part, 22 + 8 * dz + 4, sibling)

    def assemble(dz, dx):
        column = ((z + dz) % 3) * 4 + (xx + dx) % 4
        both = [all_ref[2 * column + core].astype(f32)[:SHARD_ROWS] for core in range(2)]
        at = pl.multiple_of(2 * SHARD_ROWS * column, 8)
        nat[pl.ds(at, 2 * SHARD_ROWS), :] = jnp.concatenate(both, axis=0)

    def column(dz, dx):
        for part in range(2):
            arrived(fs(dz, dx, 1), part, 22 + 8 * dz + 2 * dx)
        assemble(dz, dx)

    for part in range(2):
        turn(0, part)
    column(0, 0)
    from_z(0)
    for part in range(2):
        opposite(0, part)
    from_z(1)
    for dx in (3, 1, 2):
        column(0, dx)
    for part in range(2):
        for dz in (2, 1):
            turn(dz, part)
    for dz in (2, 1):
        column(dz, 0)

    row_in.wait()
    x = nn(by_model[...], arr[...].reshape(NF, 2 * D)).astype(bf16)
    eye = one_hot(iota((2 * D, 2 * D), 0) == iota((2 * D, 2 * D), 1))
    xt = nt(eye, x).astype(bf16)

    for part in range(2):
        for dz in (2, 1):
            opposite(dz, part)
    for dz in (2, 1):
        for dx in (3, 1):
            column(dz, dx)
    for dz in (2, 1):
        column(dz, 2)

    lin = jnp.concatenate([nat[pl.ds(q, NLC, stride=4), :] for q in range(4)], axis=1)
    lin = jnp.concatenate([lin, jnp.zeros((16, NF), f32)], axis=0).astype(bf16)
    for chunk in range(24):
        wout[:, 128 * chunk : 128 * chunk + 128] = nat[pl.ds(OUT_ROW + chunk, HID, stride=24), :].astype(bf16)
    proj_rows = nat[PROJ_ROW : PROJ_ROW + 32, :].astype(bf16)
    up = nat[UP_ROW : UP_ROW + NF * RANK, :].astype(bf16)

    r8 = one_hot(iota((8, 128), 1) % 8 == iota((8, 128), 0))
    flat_mask = iota((NF, 128), 1) // 8 == iota((NF, 128), 0) % 16
    picked = nn(one_hot(iota((NF, 32), 1) == iota((NF, 32), 0) // 16), proj_rows)
    picked = jnp.where(flat_mask, picked, 0.0).astype(bf16)
    proj_t = nt(r8, picked).astype(bf16)

    half = iota((16, 2 * D), 1) // D == iota((16, 2 * D), 0) // 8
    comp = nn(proj_t, x)
    comp = jnp.concatenate([comp, comp], axis=0)
    comp = jnp.where(half, comp, 0.0).astype(bf16)
    pair = nt(comp, x)

    def per_sample(v):
        total = jnp.sum(v.reshape(2, 8, NF), axis=(1, 2), keepdims=True) * (1.0 / (NF * RANK))
        return jnp.broadcast_to(total, (2, 8, NF)).reshape(16, NF)

    centred = pair - per_sample(pair)
    pair_scale = lax.rsqrt(per_sample(centred * centred) + 1e-05)
    normed_full = centred * pair_scale
    normed = normed_full.astype(bf16)
    row_mod = iota((16, 128), 0) % 8
    wide = jnp.concatenate(spread(normed.astype(f32), row_mod), axis=1).astype(bf16)
    preact = jnp.sum(nn(wide, up).reshape(2, 8, HID), axis=1)
    logistic = 1.0 / (1.0 + jnp.exp(-preact))
    hidden = (preact / (1.0 + jnp.exp(-preact))).astype(bf16)
    mixed = nn(hidden, wout[...])

    def by_pairs(b):
        return jnp.concatenate([lanes(mixed[b : b + 1], 384 * e, 384) for e in range(8)], axis=0)

    m0, m1 = by_pairs(0), by_pairs(1)
    mix = jnp.concatenate(
        [
            jnp.concatenate([lanes(m0, 0, D), lanes(m1, 0, D)], axis=1),
            jnp.concatenate([lanes(m0, D, D), lanes(m1, D, D)], axis=1),
        ],
        axis=0,
    )
    mix = jnp.concatenate([jnp.zeros((112, 2 * D), f32), mix], axis=0).T
    linear = nt(xt, lin)
    joined = jnp.concatenate([lanes(linear, 0, 128), lanes(linear, 128, 128) + mix], axis=1)

    joined = joined.reshape(2, D, 256)
    mean = lambda v: jnp.mean(v, axis=1, keepdims=True)
    centred_out = joined - mean(joined)
    out_scale = lax.rsqrt(mean(centred_out * centred_out) + 1e-05)
    out_normed = centred_out * out_scale
    cot = upstream[...].reshape(2, D, 256)
    d_low = out_scale * (cot - mean(cot) - out_normed * mean(cot * out_normed))
    d_low = d_low.reshape(2 * D, 256).astype(bf16)

    at = iota((272, 256), 0)
    wanted = 32 * (at % 8) + at // 8
    wanted = jnp.where(at >= 256, at - 256 + NLC, jnp.where(wanted < NLC, wanted, -1))
    d_rows = nt(one_hot(wanted == iota((272, 256), 1)), d_low)
    d_lin = rows(d_rows, 0, 256).astype(bf16)

    def by_owner_rows(v):
        return jnp.concatenate([lanes(v, 0, 128).reshape(NT, 8, 128), lanes(v, 128, 128).reshape(NT, 8, 128)], axis=1)

    halves = [by_owner_rows(nt(d_lin, rows(x, 256 * core, 256))) for core in range(2)]
    pair_out[...] = jnp.where(c == 0, halves[1], halves[0]).astype(bf16)
    kept[...] = jnp.where(c == 0, halves[0], halves[1])
    swap = pltpu.make_async_remote_copy(
        src_ref=pair_out,
        dst_ref=pair_in,
        send_sem=own_sem.at[0],
        recv_sem=own_sem.at[1],
        device_id={"fsdp": sibling},
        device_id_type=MESH,
    )
    swap.start()
    sent.append(swap)

    d_mix = rows(d_rows, 256, 16)
    d_pairs = [
        jnp.concatenate([lanes(d_mix[0:8], b * D, D), lanes(d_mix[8:16], b * D, D)], axis=1) for b in range(2)
    ]
    d_mixed = jnp.concatenate(
        [jnp.concatenate([d_pairs[b][e : e + 1] for e in range(8)], axis=1) for b in range(2)], axis=0
    )
    d_hidden = nt(d_mixed.astype(bf16), wout[...])
    d_preact = (d_hidden * logistic * (1.0 + preact * (1.0 - logistic))).astype(bf16)


    p_lane = iota((NF, NF), 1)
    to_owner = one_hot(iota((NF, NF), 0) == (p_lane % 16) * 32 + p_lane // 16)
    by_owner = jnp.concatenate(spread(nn(normed, to_owner), row_mod), axis=0).astype(bf16)
    at, source = iota((NT * 8, NF), 0), iota((NT * 8, NF), 1)
    first = nn(one_hot((at // 8 == source // 16) & (at % 8 == (source // 8) % 2)), by_owner)
    zero = jnp.zeros((2, HID), f32)
    tile = jnp.concatenate([zero, hidden.astype(f32), zero, zero], axis=0)
    first = first.reshape(NT, 8, HID) + tile[None]
    chunks = jnp.concatenate([lanes(d_pairs[b], 128 * q, 128) for b in range(2) for q in range(3)], axis=0)
    at, source = iota((NT * 8, 48), 0), iota((NT * 8, 48), 1)
    mine_here = (24 * (at % 8 - 2) + 8 * ((at // 8) % 3) + at // 24 == source) & (at % 8 >= 2) & (at % 8 < 4) & (at < 192)
    second = nn(one_hot(mine_here), chunks.astype(bf16))
    tile = jnp.concatenate([d_preact.astype(f32), zero, zero, zero], axis=0)
    second = second.reshape(NT, 8, HID) + tile[None]
    fac_msg[...] = jnp.concatenate([first, second], axis=1).astype(bf16)
    at = iota((NT * 8, NF), 0)
    slot, owner = at % 8, at // 8
    wanted = jnp.where((slot == 4) & (owner >= 3), owner - 3, -1)
    wanted = jnp.where((slot == 5) & (owner >= 3) & (owner <= 5), owner + 26, wanted)
    proj_place = one_hot(wanted == iota((NT * 8, NF), 1) // 16)
    swap.wait_recv()
    lin_msg[...] = (kept[...] + pair_in[...].astype(f32)).astype(bf16)
    lin_out.start()
    copies = jnp.concatenate(
        [jnp.broadcast_to(d_preact.astype(f32)[b : b + 1], (8, HID)) for b in range(2)], axis=0
    ).astype(bf16)
    d_normed = gather_back(nt(copies, up), row_mod)
    d_pair = pair_scale * (d_normed - per_sample(d_normed) - normed_full * per_sample(d_normed * normed_full))
    d_pair = d_pair.astype(bf16)

    d_comp = jnp.where(half, nn(d_pair, x), 0.0)
    d_comp = (d_comp[0:8] + d_comp[8:16]).astype(bf16)

    grad_proj = nt(d_comp, x).astype(bf16)
    flat = jnp.where(flat_mask, tn(grad_proj, r8), 0.0).astype(bf16)
    proj_rows_out = nn(proj_place, flat).reshape(NT, 8, 128)
    fac_msg[...] += jnp.concatenate([proj_rows_out, jnp.zeros((NT, 8, 128), f32)], axis=1).astype(bf16)
    fac_out.start()

    left_side = jnp.concatenate([comp, d_comp], axis=0)
    right_side = jnp.concatenate([d_pair, proj_t], axis=0)
    d_input = (tn(left_side, right_side) + nn(d_low, lin)).astype(bf16)
    back[...] = lax.dot_general(
        by_model[...], d_input, (((0,), (1,)), ((), ())), preferred_element_type=f32
    ).astype(bf16).reshape(NT, 16, 2 * D)

    got_lin[pl.ds(t, 1)] = lin_msg[pl.ds(t, 1)]
    got_fac[pl.ds(t, 1)] = fac_msg[pl.ds(t, 1)]
    rec_ref[pl.ds(t, 1)] = back[pl.ds(t, 1)]
    out_ref[...] = nt(out_normed.reshape(2 * D, 256).astype(bf16), order[...]).astype(bf16)
    result = local(out_ref, out_hbm, 5)
    result.start()
    locals_started.append(result)
    place = one_hot(iota((NFS * SLOTS, 384), 0) == block_ref[pl.ds(t, 1), :])

    lin_out.wait()
    linear = jnp.sum(got_lin[...].astype(f32), axis=0)
    fac_out.wait()
    factors = got_fac[...].astype(f32)
    first = factors[:, 0:8].reshape(NT * 8, 128)
    second = factors[:, 8:16].reshape(NT * 8, 128).astype(bf16)
    at = iota((NT * 8, 128), 0) % 8
    left_side = jnp.concatenate([jnp.where(at < 2, first, 0.0), jnp.where((at == 2) | (at == 3), first, 0.0)], axis=1)
    products = tn(left_side.astype(bf16), second)
    tail = jnp.sum(factors[:, 0:8], axis=0)[4:6]
    sums = jnp.concatenate(
        [
            products,
            jnp.where(c == 0, linear, 0.0),
            jnp.where(c == 1, linear, 0.0),
            tail,
            jnp.zeros((94, 128), f32),
        ],
        axis=0,
    ).astype(bf16)
    blocks[...] = nn(place, sums).astype(bf16).reshape(NFS, SLOTS, 128)

    to_fsdp.start()
    row_out.start()
    parts[pl.ds(f, 1)] = blocks[pl.ds(f, 1)]
    to_fsdp.wait()
    mine[...] = jnp.sum(parts[...].astype(f32), axis=0).astype(bf16)

    all_out.start()
    whole_ref[pl.ds(t, 1)] = mine[...][None]
    all_out.wait()
    row_out.wait()

    drain()


def finish_kernel(out_ref, rec_ref, whole_ref, row_ref, layer_ref, emb_ref, grad_ref):
    f = lax.axis_index("fsdp")
    layer_ref[...] = out_ref[...]
    emb_ref[:, 0] = rec_ref[:, :, 0:D]
    emb_ref[:, 1] = rec_ref[:, :, D : 2 * D]
    final = one_hot(iota((SHARD_ROWS, NT * SLOTS), 0) == row_ref[pl.ds(f, 1), :])
    grad_ref[...] = nn(final, whole_ref[...].reshape(NT * SLOTS, 128)) * (1.0 / SAMPLES)


VMEM = pl.BlockSpec(memory_space=pltpu.VMEM)
IN_HBM = pl.BlockSpec(memory_space=pltpu.HBM)
LIMIT = 40 * 1024 * 1024


def shape(dtype, *size):
    return jax.ShapeDtypeStruct(size, dtype)


def whole(looked, shard, as_row, cotangent):
    return pl.pallas_call(
        whole_kernel,
        out_shape=(shape(bf16, 2 * D, 256), shape(bf16, NT, 16, 2 * D), shape(bf16, NT, SLOTS, 128)),
        in_specs=[IN_HBM] * 5,
        out_specs=(IN_HBM, VMEM, VMEM),
        scratch_shapes=[
            pltpu.VMEM((NT, 2, 16, D), bf16),
            pltpu.VMEM((SHARD_ROWS, 128), bf16),
            pltpu.VMEM((1, NF), jnp.int32),
            pltpu.VMEM((2 * D, 256), bf16),
            pltpu.VMEM((NT, 384), jnp.int32),
            pltpu.VMEM((2 * D, 256), bf16),
            pltpu.VMEM((NT, 16, 2 * D), bf16),
            pltpu.VMEM((PIECE_ROWS, 128), bf16),
            pltpu.VMEM((NT, 16, 2 * D), bf16),
            pltpu.VMEM((NFS, PIECE_ROWS, 128), bf16),
            pltpu.VMEM((TOTAL_ROWS, 128), f32),
            pltpu.VMEM((HID, NFM * D), bf16),
            pltpu.VMEM((NF, NF), bf16),
            pltpu.VMEM((256, 256), bf16),
            pltpu.VMEM((2 * D, 256), f32),
            pltpu.VMEM((NT, 16, 128), bf16),
            pltpu.VMEM((NT, 16, 128), bf16),
            pltpu.VMEM((NT, 16, 128), f32),
            pltpu.VMEM((NT, 16, 128), bf16),
            pltpu.VMEM((NT, 16, 128), bf16),
            pltpu.VMEM((NT, 16, 2 * D), bf16),
            pltpu.VMEM((NT, 16, 128), bf16),
            pltpu.VMEM((NT, 16, 128), bf16),
            pltpu.VMEM((NFS, SLOTS, 128), bf16),
            pltpu.VMEM((NFS, SLOTS, 128), bf16),
            pltpu.VMEM((SLOTS, 128), bf16),
            pltpu.SemaphoreType.DMA((2,)),
            pltpu.SemaphoreType.DMA((6,)),
            pltpu.SemaphoreType.DMA((46,)),
            pltpu.SemaphoreType.DMA((46,)),
            pltpu.SemaphoreType.DMA((6,)),
            pltpu.SemaphoreType.DMA((6,)),
        ],
        compiler_params=pltpu.CompilerParams(collective_id=0, has_side_effects=True, vmem_limit_bytes=LIMIT),
    )(*[pltpu.with_memory_space_constraint(v, pltpu.HBM) for v in (looked, shard, as_row, cotangent, jnp.asarray(TO_BLOCK))])


def finish(out, rec, gathered):
    return pl.pallas_call(
        finish_kernel,
        out_shape=(shape(bf16, 2 * D, 256), shape(bf16, NT, 2, 16, D), shape(f32, SHARD_ROWS, 128)),
        in_specs=[VMEM] * 4,
        out_specs=(VMEM,) * 3,
        compiler_params=pltpu.CompilerParams(vmem_limit_bytes=12 * 1024 * 1024),
    )(out, rec, gathered, jnp.asarray(TO_ROW))


def shards(looked_up, assignment, flat_weights, cotangent):
    out, rec, gathered = whole(
        looked_up.reshape(NT, 2, 16, D),
        flat_weights.reshape(SHARD_ROWS, 128),
        assignment.reshape(1, NF),
        cotangent.transpose(0, 2, 1).reshape(2 * D, 256),
    )
    layer_out, emb, grad = finish(out, rec, gathered)
    return layer_out.reshape(2, D, 256).transpose(0, 2, 1), emb.reshape(2 * NT, 16, D), grad.reshape(SHARD_ROWS * 128)


def solution(mesh):
    return jax.shard_map(
        shards,
        mesh=mesh,
        in_specs=(P("fsdp", "table", None), P(), P("fsdp"), P(("fsdp", "table"), None, None)),
        out_specs=(P(("fsdp", "table"), None, None), P("fsdp", "table", None), P("fsdp")),
        check_vma=False,
    )
```

```python
import functools

import jax
import jax.numpy as jnp
import numpy as np
from jax import lax
from jax.experimental import pallas as pl
from jax.experimental.pallas import tpu as pltpu
from jax.sharding import PartitionSpec as P

NF = 512
D = 192
RANK = 8
HID = 128
NFM = 16
NLC = 240
NT = 32
NFS = 24
PROJ_F = 2
SHARD_ROWS = 340
PIECE_ROWS = 352
HALF_ROWS = PIECE_ROWS // 2
PROJ_ROW = 960
UP_ROW = 992
OUT_ROW = 5088
TOTAL_ROWS = 8160
SAMPLES = 1536.0
SLOTS = 16
MESH = pl.DeviceIdType.MESH
f32 = jnp.float32
bf16 = jnp.bfloat16


def _tables():
    owned = [[] for _ in range(NT)]
    for t in range(NT):
        for m in range(16):
            for k in range(8):
                owned[t].append((UP_ROW + 8 * (32 * m + t) + k, m * 8 + k))
        if t < 24:
            for h in range(HID):
                owned[t].append((OUT_ROW + 24 * h + t, 128 + h))
        for q in range(4):
            for m in range(8):
                if 32 * m + t < NLC:
                    owned[t].append((4 * (32 * m + t) + q, 256 + q * 8 + m))
    to_block = np.full((NT, 384), -1, np.int32)
    to_row = np.full((NFS, NT * SLOTS), -1, np.int32)
    seen = 0
    for t in range(NT):
        filled = [0] * NFS
        for row, place in sorted(owned[t]):
            f = row // SHARD_ROWS
            slot = filled[f]
            filled[f] += 1
            assert slot < SLOTS
            to_block[t, place] = f * SLOTS + slot
            to_row[f, t * SLOTS + slot] = row - f * SHARD_ROWS
            seen += 1
    assert seen == TOTAL_ROWS - 32
    return to_block, to_row


TO_BLOCK, TO_ROW = _tables()


def iota(shape, dim):
    return lax.broadcasted_iota(jnp.int32, shape, dim)


def one_hot(condition):
    return jnp.where(condition, 1.0, 0.0).astype(bf16)


def nn(a, b):
    return lax.dot_general(a, b, (((1,), (0,)), ((), ())), preferred_element_type=f32)


def nt(a, b):
    return lax.dot_general(a, b, (((1,), (1,)), ((), ())), preferred_element_type=f32)


def tn(a, b):
    return lax.dot_general(a, b, (((0,), (0,)), ((), ())), preferred_element_type=f32)


def lanes(x, start, size):
    return lax.slice_in_dim(x, start, start + size, axis=1)


def rows(x, start, size):
    return lax.slice_in_dim(x, start, start + size, axis=0)


def spread(values, row_mod):
    lane = iota((16, 128), 1)
    keep = lane % 8 == row_mod
    out = []
    for v in range(32):
        source = lanes(values, 128 * (v // 8), 128)
        taken = jnp.take_along_axis(source, 16 * (v % 8) + lane // 8, axis=1)
        out.append(jnp.where(keep, taken, 0.0))
    return out


def gather_back(wide, row_mod):
    lane = iota((16, 128), 1)
    index = 8 * (lane % 16) + row_mod
    out = []
    for u in range(4):
        total = jnp.zeros((16, 128), f32)
        for w in range(8):
            taken = jnp.take_along_axis(lanes(wide, 128 * (8 * u + w), 128), index, axis=1)
            total = jnp.where(lane // 16 == w, taken, total)
        out.append(total)
    return jnp.concatenate(out, axis=1)


def whole_kernel(
    lk_hbm, w_hbm, as_row_hbm, cot_hbm, block_hbm, out_hbm, rec_ref, whole_ref, proj_all,
    lk_ref, w_ref, as_row_ref, cot_ref, block_ref, out_ref, pack, padded, arr, all_ref, nat, wout, by_model, order, upstream, to_owner, owner_sum, mixed_place, linear_place, block_place, pair_out, pair_in, kept, lin_msg, fac_msg, back,
    got_lin, got_fac, blocks, parts, mine, proj_mine, proj_parts, proj_sum,
    own_sem, in_sem, proj_sem, w_send, w_recv, ex_send, ex_recv,
):
    t = lax.axis_index("table")
    f = lax.axis_index("fsdp")
    z, xx, c = f // 8, (f // 2) % 4, f % 2

    def fs(dz, dx, dc):
        return ((z + dz) % 3) * 8 + ((xx + dx) % 4) * 2 + (c + dc) % 2

    def each(n, act, first=1):
        def step(s, carry):
            act(s)
            return carry

        lax.fori_loop(first, n, step, 0)

    class Exchange:
        def __init__(self, axis, src, dst, index):
            me, self.n = (t, NT) if axis == "table" else (f, NFS)

            def copy(s):
                to = (me + s) % self.n
                return pltpu.make_async_remote_copy(
                    src_ref=src.at[to] if len(src.shape) == len(dst.shape) else src,
                    dst_ref=dst.at[me],
                    send_sem=ex_send.at[index],
                    recv_sem=ex_recv.at[index],
                    device_id={axis: to},
                    device_id_type=MESH,
                )

            self.copy = copy
            every = dst.at[pl.ds(0, self.n - 1)]
            self.every = lambda: pltpu.make_async_remote_copy(
                src_ref=every,
                dst_ref=every,
                send_sem=ex_send.at[index],
                recv_sem=ex_recv.at[index],
                device_id={axis: me},
                device_id_type=MESH,
            )

        def start(self):
            each(self.n, lambda s: self.copy(s).start())
            started.append(self)

        def wait(self):
            self.every().wait_recv()
            received.append(self)

        def wait_send(self):
            self.every().wait_send()

    started = []
    received = []
    row_in = Exchange("table", pack, arr, 0)
    lin_out = Exchange("table", lin_msg, got_lin, 1)
    fac_out = Exchange("table", fac_msg, got_fac, 2)
    row_out = Exchange("table", back, rec_ref, 3)
    all_out = Exchange("table", mine, whole_ref, 4)
    to_fsdp = Exchange("fsdp", blocks, parts, 5)
    proj_bcast = Exchange("table", proj_sum, proj_all, 6)

    def local(src, dst, index):
        return pltpu.make_async_copy(src, dst, in_sem.at[index])

    barrier = pltpu.get_barrier_semaphore()
    near = (fs(1, 0, 0), fs(2, 0, 0), fs(0, 1, 0), fs(0, 3, 0), fs(0, 0, 1))

    def greet(axis, to):
        pl.semaphore_signal(barrier, inc=1, device_id={axis: to}, device_id_type=MESH)

    greet("fsdp", near[0])
    greet("fsdp", near[1])
    for low, high in ((12, 21), (6, 12), (21, 27), (1, 6), (27, NT)):
        each(high, lambda s: greet("table", (t + s) % NT), low)
    for other in near[2:]:
        greet("fsdp", other)

    inputs = [
        local(w_hbm, w_ref, 0),
        local(lk_hbm, lk_ref, 1),
        local(as_row_hbm, as_row_ref, 2),
        local(cot_hbm, cot_ref, 3),
        local(block_hbm, block_ref, 4),
    ]
    for copy in inputs:
        copy.start()

    inputs[0].wait()
    padded[0:SHARD_ROWS] = w_ref[...]
    padded[SHARD_ROWS:PIECE_ROWS] = jnp.zeros((PIECE_ROWS - SHARD_ROWS, 128), bf16)
    inputs[1].wait()
    pack[:, :, 0:D] = lk_ref[:, 0]
    pack[:, :, D : 2 * D] = lk_ref[:, 1]
    pl.semaphore_wait(barrier, NT - 1 + len(near))

    def piece(src, shard, part, index, to):
        at = pl.ds(part * HALF_ROWS, HALF_ROWS)
        return pltpu.make_async_remote_copy(
            src_ref=src.at[at],
            dst_ref=all_ref.at[shard, at],
            send_sem=w_send.at[index],
            recv_sem=w_recv.at[index],
            device_id={"fsdp": to},
            device_id_type=MESH,
        )

    sent = []
    locals_started = []

    def drain():
        for copy in locals_started:
            copy.wait()
        for copy in sent:
            copy.wait_send()
        for exchange in started:
            if exchange not in received:
                exchange.wait()
        for exchange in started:
            exchange.wait_send()

    def send(*args):
        copy = piece(*args)
        copy.start()
        sent.append(copy)

    def forward(shard, part, index, to):
        send(all_ref.at[shard], shard, part, index + part, to)

    def arrived(shard, part, index):
        piece(all_ref.at[shard], shard, part, index + part, f).wait_recv()

    up_z, down_z, right, left, sibling = near
    for part in range(2):
        send(padded, f, part, part, up_z)
        send(padded, f, part, 2 + part, down_z)
    for part in range(2):
        send(padded, f, part, 4 + part, right)
        send(padded, f, part, 10 + part, left)
        send(padded, f, part, 22 + part, sibling)
    row_in.start()
    all_ref[pl.ds(f, 1)] = padded[...][None]
    arr[pl.ds(t, 1)] = pack[pl.ds(t, 1)]

    for copy in inputs[2:]:
        copy.wait()
    by_model[...] = one_hot(as_row_ref[...] == iota((NF, NF), 0))
    lane = iota((256, 256), 1)
    here = jnp.where(lane < NLC, lane + NFM, 2 * ((lane - NLC) % 8) + (lane - NLC) // 8)
    order[...] = one_hot(here == iota((256, 256), 0))
    upstream[...] = nn(cot_ref[...], order[...])

    def from_z(part):
        for index, dz in ((0, 2), (2, 1)):
            shard = fs(dz, 0, 0)
            arrived(shard, part, index)
            forward(shard, part, 4 + 2 * dz, right)
            forward(shard, part, 10 + 2 * dz, left)
            forward(shard, part, 22 + 8 * dz, sibling)

    def turn(dz, part):
        shard = fs(dz, 3, 0)
        arrived(shard, part, 4 + 2 * dz)
        if part == 0:
            forward(shard, part, 16 + 2 * dz, right)
        forward(shard, part, 22 + 8 * dz + 6, sibling)
        shard = fs(dz, 1, 0)
        arrived(shard, part, 10 + 2 * dz)
        if part == 1:
            forward(shard, part, 16 + 2 * dz, left)
        forward(shard, part, 22 + 8 * dz + 2, sibling)

    def opposite(dz, part):
        shard = fs(dz, 2, 0)
        arrived(shard, part, 16 + 2 * dz)
        forward(shard, part, 22 + 8 * dz + 4, sibling)

    def assemble(dz, dx):
        column = ((z + dz) % 3) * 4 + (xx + dx) % 4
        both = [all_ref[2 * column + core].astype(f32)[:SHARD_ROWS] for core in range(2)]
        at = pl.multiple_of(2 * SHARD_ROWS * column, 8)
        nat[pl.ds(at, 2 * SHARD_ROWS), :] = jnp.concatenate(both, axis=0)

    def column(dz, dx):
        for part in range(2):
            arrived(fs(dz, dx, 1), part, 22 + 8 * dz + 2 * dx)
        assemble(dz, dx)

    for part in range(2):
        turn(0, part)
    column(0, 0)

    p_lane = iota((NF, NF), 1)
    to_owner[...] = one_hot(iota((NF, NF), 0) == (p_lane % 16) * 32 + p_lane // 16)
    at, source = iota((NT * 8, NF), 0), iota((NT * 8, NF), 1)
    owner_sum[...] = one_hot((at // 8 == source // 16) & (at % 8 == (source // 8) % 2))
    at, source = iota((NT * 8, 48), 0), iota((NT * 8, 48), 1)
    mine_here = (24 * (at % 8 - 2) + 8 * ((at // 8) % 3) + at // 24 == source) & (at % 8 >= 2) & (at % 8 < 4) & (at < 192)
    mixed_place[...] = one_hot(mine_here)
    at = iota((256, 256), 0)
    wanted = 32 * (at % 8) + at // 8
    linear_place[...] = one_hot(jnp.where(wanted < NLC, wanted, -1) == iota((256, 256), 1))
    block_place[...] = one_hot(iota((NFS * SLOTS, 384), 0) == block_ref[pl.ds(t, 1), :])

    from_z(0)
    for part in range(2):
        opposite(0, part)
    from_z(1)
    for dx in (3, 1, 2):
        column(0, dx)
    for part in range(2):
        for dz in (2, 1):
            turn(dz, part)
    for dz in (2, 1):
        column(dz, 0)

    row_in.wait()
    x = nn(by_model[...], arr[...].reshape(NF, 2 * D)).astype(bf16)
    eye = one_hot(iota((2 * D, 2 * D), 0) == iota((2 * D, 2 * D), 1))
    xt = nt(eye, x).astype(bf16)

    for part in range(2):
        for dz in (2, 1):
            opposite(dz, part)
    for dz in (2, 1):
        for dx in (3, 1):
            column(dz, dx)
    for dz in (2, 1):
        column(dz, 2)

    lin = jnp.concatenate([nat[pl.ds(q, NLC, stride=4), :] for q in range(4)], axis=1)
    lin = jnp.concatenate([lin, jnp.zeros((16, NF), f32)], axis=0).astype(bf16)
    def normalise(v, c):
        v, c = v.reshape(2, D, -1), c.reshape(2, D, -1)
        mean = lambda u: jnp.mean(u, axis=1, keepdims=True)
        centred_v = v - mean(v)
        scale = lax.rsqrt(mean(centred_v * centred_v) + 1e-05)
        n = centred_v * scale
        d = scale * (c - mean(c) - n * mean(c * n))
        return n.reshape(2 * D, -1).astype(bf16), d.reshape(2 * D, -1).astype(bf16)

    linear_out, d_linear = normalise(nt(xt, lin), upstream[...])
    d_lin = nt(linear_place[...], d_linear).astype(bf16)

    def by_owner_rows(v):
        return jnp.concatenate([lanes(v, 0, 128).reshape(NT, 8, 128), lanes(v, 128, 128).reshape(NT, 8, 128)], axis=1)

    halves = [by_owner_rows(nt(d_lin, rows(x, 256 * core, 256))) for core in range(2)]
    pair_out[...] = jnp.where(c == 0, halves[1], halves[0]).astype(bf16)
    kept[...] = jnp.where(c == 0, halves[0], halves[1])
    swap = pltpu.make_async_remote_copy(
        src_ref=pair_out,
        dst_ref=pair_in,
        send_sem=own_sem.at[0],
        recv_sem=own_sem.at[1],
        device_id={"fsdp": sibling},
        device_id_type=MESH,
    )
    swap.start()
    sent.append(swap)

    for chunk in range(24):
        wout[:, 128 * chunk : 128 * chunk + 128] = nat[pl.ds(OUT_ROW + chunk, HID, stride=24), :].astype(bf16)
    proj_rows = nat[PROJ_ROW : PROJ_ROW + 32, :].astype(bf16)
    up = nat[UP_ROW : UP_ROW + NF * RANK, :].astype(bf16)

    swap.wait_recv()
    lin_msg[...] = (kept[...] + pair_in[...].astype(f32)).astype(bf16)
    lin_out.start()

    r8 = one_hot(iota((8, 128), 1) % 8 == iota((8, 128), 0))
    flat_mask = iota((NF, 128), 1) // 8 == iota((NF, 128), 0) % 16
    picked = nn(one_hot(iota((NF, 32), 1) == iota((NF, 32), 0) // 16), proj_rows)
    picked = jnp.where(flat_mask, picked, 0.0).astype(bf16)
    proj_t = nt(r8, picked).astype(bf16)

    half = iota((16, 2 * D), 1) // D == iota((16, 2 * D), 0) // 8
    comp = nn(proj_t, x)
    comp = jnp.concatenate([comp, comp], axis=0)
    comp = jnp.where(half, comp, 0.0).astype(bf16)
    pair = nt(comp, x)

    def per_sample(v):
        total = jnp.sum(v.reshape(2, 8, NF), axis=(1, 2), keepdims=True) * (1.0 / (NF * RANK))
        return jnp.broadcast_to(total, (2, 8, NF)).reshape(16, NF)

    centred = pair - per_sample(pair)
    pair_scale = lax.rsqrt(per_sample(centred * centred) + 1e-05)
    normed_full = centred * pair_scale
    normed = normed_full.astype(bf16)
    row_mod = iota((16, 128), 0) % 8
    wide = jnp.concatenate(spread(normed.astype(f32), row_mod), axis=1).astype(bf16)
    preact = jnp.sum(nn(wide, up).reshape(2, 8, HID), axis=1)
    logistic = 1.0 / (1.0 + jnp.exp(-preact))
    hidden = (preact / (1.0 + jnp.exp(-preact))).astype(bf16)
    mixed = nn(hidden, wout[...])

    def by_pairs(b):
        return jnp.concatenate([lanes(mixed[b : b + 1], 384 * e, 384) for e in range(8)], axis=0)

    m0, m1 = by_pairs(0), by_pairs(1)
    mix = jnp.concatenate(
        [
            jnp.concatenate([lanes(m0, 0, D), lanes(m1, 0, D)], axis=1),
            jnp.concatenate([lanes(m0, D, D), lanes(m1, D, D)], axis=1),
        ],
        axis=0,
    )
    mix = jnp.concatenate([jnp.zeros((112, 2 * D), f32), mix], axis=0).T
    mixed_out, d_mix = normalise(mix, lanes(upstream[...], 128, 128))
    late = iota((2 * D, 128), 1) >= 112

    def join(a, b):
        high = jnp.where(late, b.astype(f32), lanes(a, 128, 128).astype(f32)).astype(bf16)
        return jnp.concatenate([lanes(a, 0, 128), high], axis=1)

    d_low = join(d_linear, d_mix)
    d_mix = nt(one_hot(iota((16, 128), 1) == iota((16, 128), 0) + 112), d_mix)
    d_pairs = [
        jnp.concatenate([lanes(d_mix[0:8], b * D, D), lanes(d_mix[8:16], b * D, D)], axis=1) for b in range(2)
    ]
    d_mixed = jnp.concatenate(
        [jnp.concatenate([d_pairs[b][e : e + 1] for e in range(8)], axis=1) for b in range(2)], axis=0
    )
    d_hidden = nt(d_mixed.astype(bf16), wout[...])
    d_preact = (d_hidden * logistic * (1.0 + preact * (1.0 - logistic))).astype(bf16)


    by_owner = jnp.concatenate(spread(nn(normed, to_owner[...]), row_mod), axis=0).astype(bf16)
    first = nn(owner_sum[...], by_owner)
    zero = jnp.zeros((2, HID), f32)
    tile = jnp.concatenate([zero, hidden.astype(f32), zero, zero], axis=0)
    first = first.reshape(NT, 8, HID) + tile[None]
    chunks = jnp.concatenate([lanes(d_pairs[b], 128 * q, 128) for b in range(2) for q in range(3)], axis=0)
    second = nn(mixed_place[...], chunks.astype(bf16))
    tile = jnp.concatenate([d_preact.astype(f32), zero, zero, zero], axis=0)
    second = second.reshape(NT, 8, HID) + tile[None]
    fac_msg[...] = jnp.concatenate([first, second], axis=1).astype(bf16)
    fac_out.start()

    copies = jnp.concatenate(
        [jnp.broadcast_to(d_preact.astype(f32)[b : b + 1], (8, HID)) for b in range(2)], axis=0
    ).astype(bf16)
    d_normed = gather_back(nt(copies, up), row_mod)
    d_pair = pair_scale * (d_normed - per_sample(d_normed) - normed_full * per_sample(d_normed * normed_full))
    d_pair = d_pair.astype(bf16)

    d_comp = jnp.where(half, nn(d_pair, x), 0.0)
    d_comp = (d_comp[0:8] + d_comp[8:16]).astype(bf16)

    grad_proj = nt(d_comp, x).astype(bf16)
    flat = jnp.where(flat_mask, tn(grad_proj, r8), 0.0).astype(bf16)
    proj_mine[...] = nn(one_hot(iota((32, NF), 1) // 16 == iota((32, NF), 0)), flat).astype(bf16)
    proj_out = pltpu.make_async_remote_copy(
        src_ref=proj_mine,
        dst_ref=proj_parts.at[f],
        send_sem=proj_sem.at[0],
        recv_sem=proj_sem.at[1],
        device_id={"fsdp": PROJ_F},
        device_id_type=MESH,
    )

    @pl.when(f != PROJ_F)
    def _():
        proj_out.start()
        proj_all[...] = jnp.zeros_like(proj_all)

    left_side = jnp.concatenate([comp, d_comp], axis=0)
    right_side = jnp.concatenate([d_pair, proj_t], axis=0)
    d_input = (tn(left_side, right_side) + nn(d_low, lin)).astype(bf16)
    back[...] = lax.dot_general(
        by_model[...], d_input, (((0,), (1,)), ((), ())), preferred_element_type=f32
    ).astype(bf16).reshape(NT, 16, 2 * D)

    got_lin[pl.ds(t, 1)] = lin_msg[pl.ds(t, 1)]
    got_fac[pl.ds(t, 1)] = fac_msg[pl.ds(t, 1)]
    rec_ref[pl.ds(t, 1)] = back[pl.ds(t, 1)]
    out_ref[...] = nt(join(linear_out, mixed_out), order[...]).astype(bf16)
    result = local(out_ref, out_hbm, 5)
    result.start()
    locals_started.append(result)

    lin_out.wait()
    linear = jnp.sum(got_lin[...].astype(f32), axis=0)
    fac_out.wait()
    factors = got_fac[...].astype(f32)
    first = factors[:, 0:8].reshape(NT * 8, 128)
    second = factors[:, 8:16].reshape(NT * 8, 128).astype(bf16)
    at = iota((NT * 8, 128), 0) % 8
    left_side = jnp.concatenate([jnp.where(at < 2, first, 0.0), jnp.where((at == 2) | (at == 3), first, 0.0)], axis=1)
    products = tn(left_side.astype(bf16), second)
    sums = jnp.concatenate(
        [
            products,
            jnp.where(c == 0, linear, 0.0),
            jnp.where(c == 1, linear, 0.0),
            jnp.zeros((96, 128), f32),
        ],
        axis=0,
    ).astype(bf16)
    blocks[...] = nn(block_place[...], sums).astype(bf16).reshape(NFS, SLOTS, 128)

    to_fsdp.start()
    row_out.start()

    @pl.when(f == PROJ_F)
    def _():
        others = proj_parts.at[pl.ds(0, NFS - 1)]
        pltpu.make_async_remote_copy(
            src_ref=others,
            dst_ref=others,
            send_sem=proj_sem.at[0],
            recv_sem=proj_sem.at[1],
            device_id={"fsdp": f},
            device_id_type=MESH,
        ).wait_recv()
        proj_parts[pl.ds(f, 1)] = proj_mine[...][None]
        proj_sum[...] = jnp.sum(proj_parts[...].astype(f32), axis=0).astype(bf16)
        each(NT, lambda s: proj_bcast.copy(s).start())
        proj_all[pl.ds(t, 1)] = proj_sum[...][None]

    parts[pl.ds(f, 1)] = blocks[pl.ds(f, 1)]
    to_fsdp.wait()
    mine[...] = jnp.sum(parts[...].astype(f32), axis=0).astype(bf16)

    all_out.start()
    whole_ref[pl.ds(t, 1)] = mine[...][None]
    all_out.wait()
    row_out.wait()

    @pl.when(f == PROJ_F)
    def _():
        proj_bcast.wait()
        proj_bcast.wait_send()

    @pl.when(f != PROJ_F)
    def _():
        proj_out.wait_send()

    drain()


def finish_kernel(out_ref, rec_ref, whole_ref, proj_ref, row_ref, layer_ref, emb_ref, grad_ref):
    f = lax.axis_index("fsdp")
    layer_ref[...] = out_ref[...]
    emb_ref[:, 0] = rec_ref[:, :, 0:D]
    emb_ref[:, 1] = rec_ref[:, :, D : 2 * D]
    final = one_hot(iota((SHARD_ROWS, NT * SLOTS), 0) == row_ref[pl.ds(f, 1), :])
    grad_ref[...] = nn(final, whole_ref[...].reshape(NT * SLOTS, 128)) * (1.0 / SAMPLES)

    @pl.when(f == PROJ_F)
    def _():
        at = pl.ds(PROJ_ROW - PROJ_F * SHARD_ROWS, 32)
        grad_ref[at, :] = jnp.sum(proj_ref[...].astype(f32), axis=0) * (1.0 / SAMPLES)


VMEM = pl.BlockSpec(memory_space=pltpu.VMEM)
IN_HBM = pl.BlockSpec(memory_space=pltpu.HBM)
LIMIT = 40 * 1024 * 1024


def shape(dtype, *size):
    return jax.ShapeDtypeStruct(size, dtype)


def whole(looked, shard, as_row, cotangent):
    return pl.pallas_call(
        whole_kernel,
        out_shape=(
            shape(bf16, 2 * D, 256),
            shape(bf16, NT, 16, 2 * D),
            shape(bf16, NT, SLOTS, 128),
            shape(bf16, NT, 32, 128),
        ),
        in_specs=[IN_HBM] * 5,
        out_specs=(IN_HBM, VMEM, VMEM, VMEM),
        scratch_shapes=[
            pltpu.VMEM((NT, 2, 16, D), bf16),
            pltpu.VMEM((SHARD_ROWS, 128), bf16),
            pltpu.VMEM((1, NF), jnp.int32),
            pltpu.VMEM((2 * D, 256), bf16),
            pltpu.VMEM((NT, 384), jnp.int32),
            pltpu.VMEM((2 * D, 256), bf16),
            pltpu.VMEM((NT, 16, 2 * D), bf16),
            pltpu.VMEM((PIECE_ROWS, 128), bf16),
            pltpu.VMEM((NT, 16, 2 * D), bf16),
            pltpu.VMEM((NFS, PIECE_ROWS, 128), bf16),
            pltpu.VMEM((TOTAL_ROWS, 128), f32),
            pltpu.VMEM((HID, NFM * D), bf16),
            pltpu.VMEM((NF, NF), bf16),
            pltpu.VMEM((256, 256), bf16),
            pltpu.VMEM((2 * D, 256), f32),
            pltpu.VMEM((NF, NF), bf16),
            pltpu.VMEM((NT * 8, NF), bf16),
            pltpu.VMEM((NT * 8, 48), bf16),
            pltpu.VMEM((256, 256), bf16),
            pltpu.VMEM((NFS * SLOTS, 384), bf16),
            pltpu.VMEM((NT, 16, 128), bf16),
            pltpu.VMEM((NT, 16, 128), bf16),
            pltpu.VMEM((NT, 16, 128), f32),
            pltpu.VMEM((NT, 16, 128), bf16),
            pltpu.VMEM((NT, 16, 128), bf16),
            pltpu.VMEM((NT, 16, 2 * D), bf16),
            pltpu.VMEM((NT, 16, 128), bf16),
            pltpu.VMEM((NT, 16, 128), bf16),
            pltpu.VMEM((NFS, SLOTS, 128), bf16),
            pltpu.VMEM((NFS, SLOTS, 128), bf16),
            pltpu.VMEM((SLOTS, 128), bf16),
            pltpu.VMEM((32, 128), bf16),
            pltpu.VMEM((NFS, 32, 128), bf16),
            pltpu.VMEM((32, 128), bf16),
            pltpu.SemaphoreType.DMA((2,)),
            pltpu.SemaphoreType.DMA((6,)),
            pltpu.SemaphoreType.DMA((2,)),
            pltpu.SemaphoreType.DMA((46,)),
            pltpu.SemaphoreType.DMA((46,)),
            pltpu.SemaphoreType.DMA((7,)),
            pltpu.SemaphoreType.DMA((7,)),
        ],
        compiler_params=pltpu.CompilerParams(collective_id=0, has_side_effects=True, vmem_limit_bytes=LIMIT),
    )(*[pltpu.with_memory_space_constraint(v, pltpu.HBM) for v in (looked, shard, as_row, cotangent, jnp.asarray(TO_BLOCK))])


def finish(out, rec, gathered, proj):
    return pl.pallas_call(
        finish_kernel,
        out_shape=(shape(bf16, 2 * D, 256), shape(bf16, NT, 2, 16, D), shape(f32, SHARD_ROWS, 128)),
        in_specs=[VMEM] * 5,
        out_specs=(VMEM,) * 3,
        compiler_params=pltpu.CompilerParams(vmem_limit_bytes=12 * 1024 * 1024),
    )(out, rec, gathered, proj, jnp.asarray(TO_ROW))


def shards(looked_up, assignment, flat_weights, cotangent):
    out, rec, gathered, proj = whole(
        looked_up.reshape(NT, 2, 16, D),
        flat_weights.reshape(SHARD_ROWS, 128),
        assignment.reshape(1, NF),
        cotangent.transpose(0, 2, 1).reshape(2 * D, 256),
    )
    layer_out, emb, grad = finish(out, rec, gathered, proj)
    return layer_out.reshape(2, D, 256).transpose(0, 2, 1), emb.reshape(2 * NT, 16, D), grad.reshape(SHARD_ROWS * 128)


def solution(mesh):
    return jax.shard_map(
        shards,
        mesh=mesh,
        in_specs=(P("fsdp", "table", None), P(), P("fsdp"), P(("fsdp", "table"), None, None)),
        out_specs=(P(("fsdp", "table"), None, None), P("fsdp", "table", None), P("fsdp")),
        check_vma=False,
    )
```

```python
import functools

import jax
import jax.numpy as jnp
import numpy as np
from jax import lax
from jax.experimental import pallas as pl
from jax.experimental.pallas import tpu as pltpu
from jax.sharding import PartitionSpec as P

NF = 512
D = 192
RANK = 8
HID = 128
NFM = 16
NLC = 240
NT = 32
NFS = 24
PROJ_F = 2
SHARD_ROWS = 340
PIECE_ROWS = 352
HALF_ROWS = PIECE_ROWS // 2
PROJ_ROW = 960
UP_ROW = 992
OUT_ROW = 5088
TOTAL_ROWS = 8160
SAMPLES = 1536.0
SLOTS = 16
MESH = pl.DeviceIdType.MESH
f32 = jnp.float32
bf16 = jnp.bfloat16


def _tables():
    owned = [[] for _ in range(NT)]
    for t in range(NT):
        for m in range(16):
            for k in range(8):
                owned[t].append((UP_ROW + 8 * (32 * m + t) + k, m * 8 + k))
        if t < 24:
            for h in range(HID):
                owned[t].append((OUT_ROW + 24 * h + t, 128 + h))
        for q in range(4):
            for m in range(8):
                if 32 * m + t < NLC:
                    owned[t].append((4 * (32 * m + t) + q, 256 + q * 8 + m))
    to_block = np.full((NT, 384), -1, np.int32)
    to_row = np.full((NFS, NT * SLOTS), -1, np.int32)
    seen = 0
    for t in range(NT):
        filled = [0] * NFS
        for row, place in sorted(owned[t]):
            f = row // SHARD_ROWS
            slot = filled[f]
            filled[f] += 1
            assert slot < SLOTS
            to_block[t, place] = f * SLOTS + slot
            to_row[f, t * SLOTS + slot] = row - f * SHARD_ROWS
            seen += 1
    assert seen == TOTAL_ROWS - 32
    return to_block, to_row


TO_BLOCK, TO_ROW = _tables()


def iota(shape, dim):
    return lax.broadcasted_iota(jnp.int32, shape, dim)


def one_hot(condition):
    return jnp.where(condition, 1.0, 0.0).astype(bf16)


def nn(a, b):
    return lax.dot_general(a, b, (((1,), (0,)), ((), ())), preferred_element_type=f32)


def nt(a, b):
    return lax.dot_general(a, b, (((1,), (1,)), ((), ())), preferred_element_type=f32)


def tn(a, b):
    return lax.dot_general(a, b, (((0,), (0,)), ((), ())), preferred_element_type=f32)


def lanes(x, start, size):
    return lax.slice_in_dim(x, start, start + size, axis=1)


def rows(x, start, size):
    return lax.slice_in_dim(x, start, start + size, axis=0)


def spread(values, row_mod):
    lane = iota((16, 128), 1)
    keep = lane % 8 == row_mod
    out = []
    for v in range(32):
        source = lanes(values, 128 * (v // 8), 128)
        taken = jnp.take_along_axis(source, 16 * (v % 8) + lane // 8, axis=1)
        out.append(jnp.where(keep, taken, 0.0))
    return out


def gather_back(wide, row_mod):
    lane = iota((16, 128), 1)
    index = 8 * (lane % 16) + row_mod
    out = []
    for u in range(4):
        total = jnp.zeros((16, 128), f32)
        for w in range(8):
            taken = jnp.take_along_axis(lanes(wide, 128 * (8 * u + w), 128), index, axis=1)
            total = jnp.where(lane // 16 == w, taken, total)
        out.append(total)
    return jnp.concatenate(out, axis=1)


def whole_kernel(
    lk_hbm, w_hbm, as_row_hbm, cot_hbm, block_hbm, out_hbm, rec_ref, whole_ref, proj_all,
    lk_ref, w_ref, as_row_ref, cot_ref, block_ref, out_ref, pack, padded, arr, all_ref, nat, wout, by_model, order, upstream, to_owner, owner_sum, mixed_place, linear_place, block_place, pair_out, pair_in, kept, lin_msg, fac_msg, back,
    got_lin, got_fac, blocks, parts, mine, proj_mine, proj_parts, proj_sum, proj_z, proj_y,
    line_ready, own_sem, in_sem, proj_sem, w_send, w_recv, ex_send, ex_recv,
):
    t = lax.axis_index("table")
    f = lax.axis_index("fsdp")
    z, xx, c = f // 8, (f // 2) % 4, f % 2
    ty, tz = t // 4, t % 4

    def fs(dz, dx, dc):
        return ((z + dz) % 3) * 8 + ((xx + dx) % 4) * 2 + (c + dc) % 2

    def each(n, act, first=1):
        def step(s, carry):
            act(s)
            return carry

        lax.fori_loop(first, n, step, 0)

    class Exchange:
        def __init__(self, axis, src, dst, index):
            me, self.n = (t, NT) if axis == "table" else (f, NFS)

            def copy_to(to):
                return pltpu.make_async_remote_copy(
                    src_ref=src.at[to] if len(src.shape) == len(dst.shape) else src,
                    dst_ref=dst.at[me],
                    send_sem=ex_send.at[index],
                    recv_sem=ex_recv.at[index],
                    device_id={axis: to},
                    device_id_type=MESH,
                )

            self.copy_to = copy_to
            self.copy = lambda s: copy_to((me + s) % self.n)
            every = dst.at[pl.ds(0, self.n - 1)]
            self.every = lambda: pltpu.make_async_remote_copy(
                src_ref=every,
                dst_ref=every,
                send_sem=ex_send.at[index],
                recv_sem=ex_recv.at[index],
                device_id={axis: me},
                device_id_type=MESH,
            )

        def start(self):
            each(self.n, lambda s: self.copy(s).start())
            started.append(self)

        def wait(self):
            self.every().wait_recv()
            received.append(self)

        def wait_send(self):
            self.every().wait_send()

    started = []
    received = []
    row_in = Exchange("table", pack, arr, 0)
    lin_out = Exchange("table", lin_msg, got_lin, 1)
    fac_out = Exchange("table", fac_msg, got_fac, 2)
    row_out = Exchange("table", back, rec_ref, 3)
    all_out = Exchange("table", mine, whole_ref, 4)
    to_fsdp = Exchange("fsdp", blocks, parts, 5)


    def along(src, dst, at, n, to, index):
        def copy(s):
            return pltpu.make_async_remote_copy(
                src_ref=src,
                dst_ref=dst.at[at],
                send_sem=proj_sem.at[index],
                recv_sem=proj_sem.at[index + 1],
                device_id={"table": to(s)},
                device_id_type=MESH,
            )

        every = dst.at[pl.ds(0, n - 1)]
        both = pltpu.make_async_remote_copy(
            src_ref=every,
            dst_ref=every,
            send_sem=proj_sem.at[index],
            recv_sem=proj_sem.at[index + 1],
            device_id={"table": t},
            device_id_type=MESH,
        )
        return (lambda: each(n, lambda s: copy(s).start())), both

    z_start, z_every = along(proj_sum, proj_z, tz, 4, lambda s: ty * 4 + (tz + s) % 4, 2)
    y_start, y_every = along(proj_y, proj_all, ty, 8, lambda s: ((ty + s) % 8) * 4 + tz, 4)

    def local(src, dst, index):
        return pltpu.make_async_copy(src, dst, in_sem.at[index])

    barrier = pltpu.get_barrier_semaphore()
    near = (fs(1, 0, 0), fs(2, 0, 0), fs(0, 1, 0), fs(0, 3, 0), fs(0, 0, 1))

    def greet(axis, to):
        pl.semaphore_signal(barrier, inc=1, device_id={axis: to}, device_id_type=MESH)

    greet("fsdp", near[0])
    greet("fsdp", near[1])
    for dy in (4, 3, 5, 2, 6, 1, 7):
        greet("table", ((ty + dy) % 8) * 4 + tz)
    for dz in (2, 3, 1):
        greet("table", ty * 4 + (tz + dz) % 4)
    for other in near[2:]:
        greet("fsdp", other)

    inputs = [
        local(w_hbm, w_ref, 0),
        local(lk_hbm, lk_ref, 1),
        local(as_row_hbm, as_row_ref, 2),
        local(cot_hbm, cot_ref, 3),
        local(block_hbm, block_ref, 4),
    ]
    for copy in inputs:
        copy.start()

    inputs[0].wait()
    padded[0:SHARD_ROWS] = w_ref[...]
    padded[SHARD_ROWS:PIECE_ROWS] = jnp.zeros((PIECE_ROWS - SHARD_ROWS, 128), bf16)
    inputs[1].wait()
    pack[:, :, 0:D] = lk_ref[:, 0]
    pack[:, :, D : 2 * D] = lk_ref[:, 1]
    pl.semaphore_wait(barrier, 10 + len(near))
    for dz in (2, 3, 1):
        pl.semaphore_signal(
            line_ready, inc=1, device_id={"table": ty * 4 + (tz + dz) % 4}, device_id_type=MESH
        )

    def piece(src, shard, part, index, to):
        at = pl.ds(part * HALF_ROWS, HALF_ROWS)
        return pltpu.make_async_remote_copy(
            src_ref=src.at[at],
            dst_ref=all_ref.at[shard, at],
            send_sem=w_send.at[index],
            recv_sem=w_recv.at[index],
            device_id={"fsdp": to},
            device_id_type=MESH,
        )

    sent = []
    locals_started = []

    def drain():
        for copy in locals_started:
            copy.wait()
        for copy in sent:
            copy.wait_send()
        for exchange in started:
            if exchange not in received:
                exchange.wait()
        for exchange in started:
            exchange.wait_send()

    def send(*args):
        copy = piece(*args)
        copy.start()
        sent.append(copy)

    def forward(shard, part, index, to):
        send(all_ref.at[shard], shard, part, index + part, to)

    def arrived(shard, part, index):
        piece(all_ref.at[shard], shard, part, index + part, f).wait_recv()

    up_z, down_z, right, left, sibling = near
    for part in range(2):
        send(padded, f, part, part, up_z)
        send(padded, f, part, 2 + part, down_z)
    for part in range(2):
        send(padded, f, part, 4 + part, right)
        send(padded, f, part, 10 + part, left)
        send(padded, f, part, 22 + part, sibling)
    started.append(row_in)
    for dz in range(1, 4):
        row_in.copy_to(ty * 4 + (tz + dz) % 4).start()
    each(8, lambda s: row_in.copy_to(((ty + s) % 8) * 4 + tz).start())
    all_ref[pl.ds(f, 1)] = padded[...][None]
    arr[pl.ds(t, 1)] = pack[pl.ds(t, 1)]

    for copy in inputs[2:]:
        copy.wait()
    by_model[...] = one_hot(as_row_ref[...] == iota((NF, NF), 0))
    lane = iota((256, 256), 1)
    here = jnp.where(lane < NLC, lane + NFM, 2 * ((lane - NLC) % 8) + (lane - NLC) // 8)
    order[...] = one_hot(here == iota((256, 256), 0))
    upstream[...] = nn(cot_ref[...], order[...])

    pl.semaphore_wait(line_ready, 3)
    for dz in range(1, 4):
        each(8, lambda s: row_in.copy_to(((ty + s) % 8) * 4 + (tz + dz) % 4).start())

    def from_z(part):
        for index, dz in ((0, 2), (2, 1)):
            shard = fs(dz, 0, 0)
            arrived(shard, part, index)
            forward(shard, part, 4 + 2 * dz, right)
            forward(shard, part, 10 + 2 * dz, left)
            forward(shard, part, 22 + 8 * dz, sibling)

    def turn(dz, part):
        shard = fs(dz, 3, 0)
        arrived(shard, part, 4 + 2 * dz)
        if part == 0:
            forward(shard, part, 16 + 2 * dz, right)
        forward(shard, part, 22 + 8 * dz + 6, sibling)
        shard = fs(dz, 1, 0)
        arrived(shard, part, 10 + 2 * dz)
        if part == 1:
            forward(shard, part, 16 + 2 * dz, left)
        forward(shard, part, 22 + 8 * dz + 2, sibling)

    def opposite(dz, part):
        shard = fs(dz, 2, 0)
        arrived(shard, part, 16 + 2 * dz)
        forward(shard, part, 22 + 8 * dz + 4, sibling)

    def assemble(dz, dx):
        column = ((z + dz) % 3) * 4 + (xx + dx) % 4
        both = [all_ref[2 * column + core].astype(f32)[:SHARD_ROWS] for core in range(2)]
        at = pl.multiple_of(2 * SHARD_ROWS * column, 8)
        nat[pl.ds(at, 2 * SHARD_ROWS), :] = jnp.concatenate(both, axis=0)

    def column(dz, dx):
        for part in range(2):
            arrived(fs(dz, dx, 1), part, 22 + 8 * dz + 2 * dx)
        assemble(dz, dx)

    for part in range(2):
        turn(0, part)
    column(0, 0)

    p_lane = iota((NF, NF), 1)
    to_owner[...] = one_hot(iota((NF, NF), 0) == (p_lane % 16) * 32 + p_lane // 16)
    at, source = iota((NT * 8, NF), 0), iota((NT * 8, NF), 1)
    owner_sum[...] = one_hot((at // 8 == source // 16) & (at % 8 == (source // 8) % 2))
    at, source = iota((NT * 8, 48), 0), iota((NT * 8, 48), 1)
    mine_here = (24 * (at % 8 - 2) + 8 * ((at // 8) % 3) + at // 24 == source) & (at % 8 >= 2) & (at % 8 < 4) & (at < 192)
    mixed_place[...] = one_hot(mine_here)
    at = iota((256, 256), 0)
    wanted = 32 * (at % 8) + at // 8
    linear_place[...] = one_hot(jnp.where(wanted < NLC, wanted, -1) == iota((256, 256), 1))
    block_place[...] = one_hot(iota((NFS * SLOTS, 384), 0) == block_ref[pl.ds(t, 1), :])

    from_z(0)
    for part in range(2):
        opposite(0, part)
    from_z(1)
    for dx in (3, 1, 2):
        column(0, dx)
    for part in range(2):
        for dz in (2, 1):
            turn(dz, part)
    for dz in (2, 1):
        column(dz, 0)

    row_in.wait()
    x = nn(by_model[...], arr[...].reshape(NF, 2 * D)).astype(bf16)
    eye = one_hot(iota((2 * D, 2 * D), 0) == iota((2 * D, 2 * D), 1))
    xt = nt(eye, x).astype(bf16)

    for part in range(2):
        for dz in (2, 1):
            opposite(dz, part)
    for dz in (2, 1):
        for dx in (3, 1):
            column(dz, dx)
    for dz in (2, 1):
        column(dz, 2)

    lin = jnp.concatenate([nat[pl.ds(q, NLC, stride=4), :] for q in range(4)], axis=1)
    lin = jnp.concatenate([lin, jnp.zeros((16, NF), f32)], axis=0).astype(bf16)
    def normalise(v, c):
        v, c = v.reshape(2, D, -1), c.reshape(2, D, -1)
        mean = lambda u: jnp.mean(u, axis=1, keepdims=True)
        centred_v = v - mean(v)
        scale = lax.rsqrt(mean(centred_v * centred_v) + 1e-05)
        n = centred_v * scale
        d = scale * (c - mean(c) - n * mean(c * n))
        return n.reshape(2 * D, -1).astype(bf16), d.reshape(2 * D, -1).astype(bf16)

    linear_out, d_linear = normalise(nt(xt, lin), upstream[...])
    d_lin = nt(linear_place[...], d_linear).astype(bf16)

    def by_owner_rows(v):
        return jnp.concatenate([lanes(v, 0, 128).reshape(NT, 8, 128), lanes(v, 128, 128).reshape(NT, 8, 128)], axis=1)

    halves = [by_owner_rows(nt(d_lin, rows(x, 256 * core, 256))) for core in range(2)]
    pair_out[...] = jnp.where(c == 0, halves[1], halves[0]).astype(bf16)
    kept[...] = jnp.where(c == 0, halves[0], halves[1])
    swap = pltpu.make_async_remote_copy(
        src_ref=pair_out,
        dst_ref=pair_in,
        send_sem=own_sem.at[0],
        recv_sem=own_sem.at[1],
        device_id={"fsdp": sibling},
        device_id_type=MESH,
    )
    swap.start()
    sent.append(swap)

    for chunk in range(24):
        wout[:, 128 * chunk : 128 * chunk + 128] = nat[pl.ds(OUT_ROW + chunk, HID, stride=24), :].astype(bf16)
    proj_rows = nat[PROJ_ROW : PROJ_ROW + 32, :].astype(bf16)
    up = nat[UP_ROW : UP_ROW + NF * RANK, :].astype(bf16)

    swap.wait_recv()
    lin_msg[...] = (kept[...] + pair_in[...].astype(f32)).astype(bf16)
    lin_out.start()

    r8 = one_hot(iota((8, 128), 1) % 8 == iota((8, 128), 0))
    flat_mask = iota((NF, 128), 1) // 8 == iota((NF, 128), 0) % 16
    picked = nn(one_hot(iota((NF, 32), 1) == iota((NF, 32), 0) // 16), proj_rows)
    picked = jnp.where(flat_mask, picked, 0.0).astype(bf16)
    proj_t = nt(r8, picked).astype(bf16)

    half = iota((16, 2 * D), 1) // D == iota((16, 2 * D), 0) // 8
    comp = nn(proj_t, x)
    comp = jnp.concatenate([comp, comp], axis=0)
    comp = jnp.where(half, comp, 0.0).astype(bf16)
    pair = nt(comp, x)

    def per_sample(v):
        total = jnp.sum(v.reshape(2, 8, NF), axis=(1, 2), keepdims=True) * (1.0 / (NF * RANK))
        return jnp.broadcast_to(total, (2, 8, NF)).reshape(16, NF)

    centred = pair - per_sample(pair)
    pair_scale = lax.rsqrt(per_sample(centred * centred) + 1e-05)
    normed_full = centred * pair_scale
    normed = normed_full.astype(bf16)
    row_mod = iota((16, 128), 0) % 8
    wide = jnp.concatenate(spread(normed.astype(f32), row_mod), axis=1).astype(bf16)
    preact = jnp.sum(nn(wide, up).reshape(2, 8, HID), axis=1)
    logistic = 1.0 / (1.0 + jnp.exp(-preact))
    hidden = (preact / (1.0 + jnp.exp(-preact))).astype(bf16)
    mixed = nn(hidden, wout[...])

    def by_pairs(b):
        return jnp.concatenate([lanes(mixed[b : b + 1], 384 * e, 384) for e in range(8)], axis=0)

    m0, m1 = by_pairs(0), by_pairs(1)
    mix = jnp.concatenate(
        [
            jnp.concatenate([lanes(m0, 0, D), lanes(m1, 0, D)], axis=1),
            jnp.concatenate([lanes(m0, D, D), lanes(m1, D, D)], axis=1),
        ],
        axis=0,
    )
    mix = jnp.concatenate([jnp.zeros((112, 2 * D), f32), mix], axis=0).T
    mixed_out, d_mix = normalise(mix, lanes(upstream[...], 128, 128))
    late = iota((2 * D, 128), 1) >= 112

    def join(a, b):
        high = jnp.where(late, b.astype(f32), lanes(a, 128, 128).astype(f32)).astype(bf16)
        return jnp.concatenate([lanes(a, 0, 128), high], axis=1)

    d_low = join(d_linear, d_mix)
    d_mix = nt(one_hot(iota((16, 128), 1) == iota((16, 128), 0) + 112), d_mix)
    d_pairs = [
        jnp.concatenate([lanes(d_mix[0:8], b * D, D), lanes(d_mix[8:16], b * D, D)], axis=1) for b in range(2)
    ]
    d_mixed = jnp.concatenate(
        [jnp.concatenate([d_pairs[b][e : e + 1] for e in range(8)], axis=1) for b in range(2)], axis=0
    )
    d_hidden = nt(d_mixed.astype(bf16), wout[...])
    d_preact = (d_hidden * logistic * (1.0 + preact * (1.0 - logistic))).astype(bf16)


    by_owner = jnp.concatenate(spread(nn(normed, to_owner[...]), row_mod), axis=0).astype(bf16)
    first = nn(owner_sum[...], by_owner)
    zero = jnp.zeros((2, HID), f32)
    tile = jnp.concatenate([zero, hidden.astype(f32), zero, zero], axis=0)
    first = first.reshape(NT, 8, HID) + tile[None]
    chunks = jnp.concatenate([lanes(d_pairs[b], 128 * q, 128) for b in range(2) for q in range(3)], axis=0)
    second = nn(mixed_place[...], chunks.astype(bf16))
    tile = jnp.concatenate([d_preact.astype(f32), zero, zero, zero], axis=0)
    second = second.reshape(NT, 8, HID) + tile[None]
    fac_msg[...] = jnp.concatenate([first, second], axis=1).astype(bf16)
    fac_out.start()

    copies = jnp.concatenate(
        [jnp.broadcast_to(d_preact.astype(f32)[b : b + 1], (8, HID)) for b in range(2)], axis=0
    ).astype(bf16)
    d_normed = gather_back(nt(copies, up), row_mod)
    d_pair = pair_scale * (d_normed - per_sample(d_normed) - normed_full * per_sample(d_normed * normed_full))
    d_pair = d_pair.astype(bf16)

    d_comp = jnp.where(half, nn(d_pair, x), 0.0)
    d_comp = (d_comp[0:8] + d_comp[8:16]).astype(bf16)

    grad_proj = nt(d_comp, x).astype(bf16)
    flat = jnp.where(flat_mask, tn(grad_proj, r8), 0.0).astype(bf16)
    proj_mine[...] = nn(one_hot(iota((32, NF), 1) // 16 == iota((32, NF), 0)), flat).astype(bf16)
    proj_out = pltpu.make_async_remote_copy(
        src_ref=proj_mine,
        dst_ref=proj_parts.at[f],
        send_sem=proj_sem.at[0],
        recv_sem=proj_sem.at[1],
        device_id={"fsdp": PROJ_F},
        device_id_type=MESH,
    )

    @pl.when(f != PROJ_F)
    def _():
        proj_out.start()
        proj_all[...] = jnp.zeros_like(proj_all)

    left_side = jnp.concatenate([comp, d_comp], axis=0)
    right_side = jnp.concatenate([d_pair, proj_t], axis=0)
    d_input = (tn(left_side, right_side) + nn(d_low, lin)).astype(bf16)
    back[...] = lax.dot_general(
        by_model[...], d_input, (((0,), (1,)), ((), ())), preferred_element_type=f32
    ).astype(bf16).reshape(NT, 16, 2 * D)

    got_lin[pl.ds(t, 1)] = lin_msg[pl.ds(t, 1)]
    got_fac[pl.ds(t, 1)] = fac_msg[pl.ds(t, 1)]
    rec_ref[pl.ds(t, 1)] = back[pl.ds(t, 1)]
    out_ref[...] = nt(join(linear_out, mixed_out), order[...]).astype(bf16)
    result = local(out_ref, out_hbm, 5)
    result.start()
    locals_started.append(result)

    lin_out.wait()
    linear = jnp.sum(got_lin[...].astype(f32), axis=0)
    fac_out.wait()
    factors = got_fac[...].astype(f32)
    first = factors[:, 0:8].reshape(NT * 8, 128)
    second = factors[:, 8:16].reshape(NT * 8, 128).astype(bf16)
    at = iota((NT * 8, 128), 0) % 8
    left_side = jnp.concatenate([jnp.where(at < 2, first, 0.0), jnp.where((at == 2) | (at == 3), first, 0.0)], axis=1)
    products = tn(left_side.astype(bf16), second)
    sums = jnp.concatenate(
        [
            products,
            jnp.where(c == 0, linear, 0.0),
            jnp.where(c == 1, linear, 0.0),
            jnp.zeros((96, 128), f32),
        ],
        axis=0,
    ).astype(bf16)
    blocks[...] = nn(block_place[...], sums).astype(bf16).reshape(NFS, SLOTS, 128)

    to_fsdp.start()

    @pl.when(f == PROJ_F)
    def _():
        others = proj_parts.at[pl.ds(0, NFS - 1)]
        pltpu.make_async_remote_copy(
            src_ref=others,
            dst_ref=others,
            send_sem=proj_sem.at[0],
            recv_sem=proj_sem.at[1],
            device_id={"fsdp": f},
            device_id_type=MESH,
        ).wait_recv()
        proj_parts[pl.ds(f, 1)] = proj_mine[...][None]
        proj_sum[...] = jnp.sum(proj_parts[...].astype(f32), axis=0).astype(bf16)
        z_start()
        proj_z[pl.ds(tz, 1)] = proj_sum[...][None]

    row_out.start()

    @pl.when(f == PROJ_F)
    def _():
        z_every.wait_recv()
        proj_y[...] = jnp.sum(proj_z[...].astype(f32), axis=0).astype(bf16)
        y_start()
        proj_all[pl.ds(ty, 1)] = proj_y[...][None]

    parts[pl.ds(f, 1)] = blocks[pl.ds(f, 1)]
    to_fsdp.wait()
    mine[...] = jnp.sum(parts[...].astype(f32), axis=0).astype(bf16)

    all_out.start()
    whole_ref[pl.ds(t, 1)] = mine[...][None]
    all_out.wait()
    row_out.wait()

    @pl.when(f == PROJ_F)
    def _():
        y_every.wait_recv()
        z_every.wait_send()
        y_every.wait_send()

    @pl.when(f != PROJ_F)
    def _():
        proj_out.wait_send()

    drain()


def finish_kernel(out_ref, rec_ref, whole_ref, proj_ref, row_ref, layer_ref, emb_ref, grad_ref):
    f = lax.axis_index("fsdp")
    layer_ref[...] = out_ref[...]
    emb_ref[:, 0] = rec_ref[:, :, 0:D]
    emb_ref[:, 1] = rec_ref[:, :, D : 2 * D]
    final = one_hot(iota((SHARD_ROWS, NT * SLOTS), 0) == row_ref[pl.ds(f, 1), :])
    grad_ref[...] = nn(final, whole_ref[...].reshape(NT * SLOTS, 128)) * (1.0 / SAMPLES)

    @pl.when(f == PROJ_F)
    def _():
        at = pl.ds(PROJ_ROW - PROJ_F * SHARD_ROWS, 32)
        grad_ref[at, :] = jnp.sum(proj_ref[...].astype(f32), axis=0) * (1.0 / SAMPLES)


VMEM = pl.BlockSpec(memory_space=pltpu.VMEM)
IN_HBM = pl.BlockSpec(memory_space=pltpu.HBM)
LIMIT = 40 * 1024 * 1024


def shape(dtype, *size):
    return jax.ShapeDtypeStruct(size, dtype)


def whole(looked, shard, as_row, cotangent):
    return pl.pallas_call(
        whole_kernel,
        out_shape=(
            shape(bf16, 2 * D, 256),
            shape(bf16, NT, 16, 2 * D),
            shape(bf16, NT, SLOTS, 128),
            shape(bf16, 8, 32, 128),
        ),
        in_specs=[IN_HBM] * 5,
        out_specs=(IN_HBM, VMEM, VMEM, VMEM),
        scratch_shapes=[
            pltpu.VMEM((NT, 2, 16, D), bf16),
            pltpu.VMEM((SHARD_ROWS, 128), bf16),
            pltpu.VMEM((1, NF), jnp.int32),
            pltpu.VMEM((2 * D, 256), bf16),
            pltpu.VMEM((NT, 384), jnp.int32),
            pltpu.VMEM((2 * D, 256), bf16),
            pltpu.VMEM((NT, 16, 2 * D), bf16),
            pltpu.VMEM((PIECE_ROWS, 128), bf16),
            pltpu.VMEM((NT, 16, 2 * D), bf16),
            pltpu.VMEM((NFS, PIECE_ROWS, 128), bf16),
            pltpu.VMEM((TOTAL_ROWS, 128), f32),
            pltpu.VMEM((HID, NFM * D), bf16),
            pltpu.VMEM((NF, NF), bf16),
            pltpu.VMEM((256, 256), bf16),
            pltpu.VMEM((2 * D, 256), f32),
            pltpu.VMEM((NF, NF), bf16),
            pltpu.VMEM((NT * 8, NF), bf16),
            pltpu.VMEM((NT * 8, 48), bf16),
            pltpu.VMEM((256, 256), bf16),
            pltpu.VMEM((NFS * SLOTS, 384), bf16),
            pltpu.VMEM((NT, 16, 128), bf16),
            pltpu.VMEM((NT, 16, 128), bf16),
            pltpu.VMEM((NT, 16, 128), f32),
            pltpu.VMEM((NT, 16, 128), bf16),
            pltpu.VMEM((NT, 16, 128), bf16),
            pltpu.VMEM((NT, 16, 2 * D), bf16),
            pltpu.VMEM((NT, 16, 128), bf16),
            pltpu.VMEM((NT, 16, 128), bf16),
            pltpu.VMEM((NFS, SLOTS, 128), bf16),
            pltpu.VMEM((NFS, SLOTS, 128), bf16),
            pltpu.VMEM((SLOTS, 128), bf16),
            pltpu.VMEM((32, 128), bf16),
            pltpu.VMEM((NFS, 32, 128), bf16),
            pltpu.VMEM((32, 128), bf16),
            pltpu.VMEM((4, 32, 128), bf16),
            pltpu.VMEM((32, 128), bf16),
            pltpu.SemaphoreType.REGULAR,
            pltpu.SemaphoreType.DMA((2,)),
            pltpu.SemaphoreType.DMA((6,)),
            pltpu.SemaphoreType.DMA((6,)),
            pltpu.SemaphoreType.DMA((46,)),
            pltpu.SemaphoreType.DMA((46,)),
            pltpu.SemaphoreType.DMA((6,)),
            pltpu.SemaphoreType.DMA((6,)),
        ],
        compiler_params=pltpu.CompilerParams(collective_id=0, has_side_effects=True, vmem_limit_bytes=LIMIT),
    )(*[pltpu.with_memory_space_constraint(v, pltpu.HBM) for v in (looked, shard, as_row, cotangent, jnp.asarray(TO_BLOCK))])


def finish(out, rec, gathered, proj):
    return pl.pallas_call(
        finish_kernel,
        out_shape=(shape(bf16, 2 * D, 256), shape(bf16, NT, 2, 16, D), shape(f32, SHARD_ROWS, 128)),
        in_specs=[VMEM] * 5,
        out_specs=(VMEM,) * 3,
        compiler_params=pltpu.CompilerParams(vmem_limit_bytes=12 * 1024 * 1024),
    )(out, rec, gathered, proj, jnp.asarray(TO_ROW))


def shards(looked_up, assignment, flat_weights, cotangent):
    out, rec, gathered, proj = whole(
        looked_up.reshape(NT, 2, 16, D),
        flat_weights.reshape(SHARD_ROWS, 128),
        assignment.reshape(1, NF),
        cotangent.transpose(0, 2, 1).reshape(2 * D, 256),
    )
    layer_out, emb, grad = finish(out, rec, gathered, proj)
    return layer_out.reshape(2, D, 256).transpose(0, 2, 1), emb.reshape(2 * NT, 16, D), grad.reshape(SHARD_ROWS * 128)


def solution(mesh):
    return jax.shard_map(
        shards,
        mesh=mesh,
        in_specs=(P("fsdp", "table", None), P(), P("fsdp"), P(("fsdp", "table"), None, None)),
        out_specs=(P(("fsdp", "table"), None, None), P("fsdp", "table", None), P("fsdp")),
        check_vma=False,
    )
```

```python
import functools

import jax
import jax.numpy as jnp
import numpy as np
from jax import lax
from jax.experimental import pallas as pl
from jax.experimental.pallas import tpu as pltpu
from jax.sharding import PartitionSpec as P

NF = 512
D = 192
RANK = 8
HID = 128
NFM = 16
NLC = 240
NT = 32
NFS = 24
PROJ_F = 2
SHARD_ROWS = 340
PIECE_ROWS = 352
HALF_ROWS = PIECE_ROWS // 2
PROJ_ROW = 960
UP_ROW = 992
OUT_ROW = 5088
TOTAL_ROWS = 8160
SAMPLES = 1536.0
SLOTS = 16
MESH = pl.DeviceIdType.MESH
f32 = jnp.float32
bf16 = jnp.bfloat16


def _tables():
    owned = [[] for _ in range(NT)]
    for t in range(NT):
        for m in range(16):
            for k in range(8):
                owned[t].append((UP_ROW + 8 * (32 * m + t) + k, m * 8 + k))
        if t < 24:
            for h in range(HID):
                owned[t].append((OUT_ROW + 24 * h + t, 128 + h))
        for q in range(4):
            for m in range(8):
                if 32 * m + t < NLC:
                    owned[t].append((4 * (32 * m + t) + q, 256 + q * 8 + m))
    to_block = np.full((NT, 384), -1, np.int32)
    to_row = np.full((NFS, NT * SLOTS), -1, np.int32)
    seen = 0
    for t in range(NT):
        filled = [0] * NFS
        for row, place in sorted(owned[t]):
            f = row // SHARD_ROWS
            slot = filled[f]
            filled[f] += 1
            assert slot < SLOTS
            to_block[t, place] = f * SLOTS + slot
            to_row[f, t * SLOTS + slot] = row - f * SHARD_ROWS
            seen += 1
    assert seen == TOTAL_ROWS - 32
    return to_block, to_row


TO_BLOCK, TO_ROW = _tables()


def iota(shape, dim):
    return lax.broadcasted_iota(jnp.int32, shape, dim)


def one_hot(condition):
    return jnp.where(condition, 1.0, 0.0).astype(bf16)


def nn(a, b):
    return lax.dot_general(a, b, (((1,), (0,)), ((), ())), preferred_element_type=f32)


def nt(a, b):
    return lax.dot_general(a, b, (((1,), (1,)), ((), ())), preferred_element_type=f32)


def tn(a, b):
    return lax.dot_general(a, b, (((0,), (0,)), ((), ())), preferred_element_type=f32)


def lanes(x, start, size):
    return lax.slice_in_dim(x, start, start + size, axis=1)


def rows(x, start, size):
    return lax.slice_in_dim(x, start, start + size, axis=0)


def spread(values, row_mod):
    lane = iota((16, 128), 1)
    keep = lane % 8 == row_mod
    out = []
    for v in range(32):
        source = lanes(values, 128 * (v // 8), 128)
        taken = jnp.take_along_axis(source, 16 * (v % 8) + lane // 8, axis=1)
        out.append(jnp.where(keep, taken, 0.0))
    return out


def gather_back(wide, row_mod):
    lane = iota((16, 128), 1)
    index = 8 * (lane % 16) + row_mod
    out = []
    for u in range(4):
        total = jnp.zeros((16, 128), f32)
        for w in range(8):
            taken = jnp.take_along_axis(lanes(wide, 128 * (8 * u + w), 128), index, axis=1)
            total = jnp.where(lane // 16 == w, taken, total)
        out.append(total)
    return jnp.concatenate(out, axis=1)


def whole_kernel(
    lk_hbm, w_hbm, as_row_hbm, cot_hbm, block_hbm, out_hbm, rec_ref, whole_ref, proj_all,
    lk_ref, w_ref, as_row_ref, cot_ref, block_ref, out_ref, pack, padded, arr, all_ref, nat, wout, by_model, order, upstream, to_owner, owner_sum, mixed_place, linear_place, block_place, pair_out, pair_in, kept, lin_msg, fac_msg, back,
    got_lin, got_fac, blocks, parts, mine, proj_mine, proj_parts, proj_sum, proj_z, proj_y,
    line_ready, own_sem, in_sem, proj_sem, w_send, w_recv, ex_send, ex_recv,
):
    t = lax.axis_index("table")
    f = lax.axis_index("fsdp")
    z, xx, c = f // 8, (f // 2) % 4, f % 2
    ty, tz = t // 4, t % 4

    def fs(dz, dx, dc):
        return ((z + dz) % 3) * 8 + ((xx + dx) % 4) * 2 + (c + dc) % 2

    def each(n, act, first=1):
        def step(s, carry):
            act(s)
            return carry

        lax.fori_loop(first, n, step, 0)

    class Exchange:
        def __init__(self, axis, src, dst, index):
            me, self.n = (t, NT) if axis == "table" else (f, NFS)

            def copy_to(to):
                return pltpu.make_async_remote_copy(
                    src_ref=src.at[to] if len(src.shape) == len(dst.shape) else src,
                    dst_ref=dst.at[me],
                    send_sem=ex_send.at[index],
                    recv_sem=ex_recv.at[index],
                    device_id={axis: to},
                    device_id_type=MESH,
                )

            self.order = ((12, 21), (6, 12), (21, 27), (1, 6), (27, NT)) if axis == "table" else ((8, NFS), (1, 8))
            self.copy_to = copy_to
            self.copy = lambda s: copy_to((me + s) % self.n)
            every = dst.at[pl.ds(0, self.n - 1)]
            self.every = lambda: pltpu.make_async_remote_copy(
                src_ref=every,
                dst_ref=every,
                send_sem=ex_send.at[index],
                recv_sem=ex_recv.at[index],
                device_id={axis: me},
                device_id_type=MESH,
            )

        def start(self):
            for low, high in self.order:
                each(high, lambda s: self.copy(s).start(), low)
            started.append(self)

        def wait(self):
            self.every().wait_recv()
            received.append(self)

        def wait_send(self):
            self.every().wait_send()

    started = []
    received = []
    row_in = Exchange("table", pack, arr, 0)
    lin_out = Exchange("table", lin_msg, got_lin, 1)
    fac_out = Exchange("table", fac_msg, got_fac, 2)
    row_out = Exchange("table", back, rec_ref, 3)
    all_out = Exchange("table", mine, whole_ref, 4)
    to_fsdp = Exchange("fsdp", blocks, parts, 5)


    def along(src, dst, at, n, to, index):
        def copy(s):
            return pltpu.make_async_remote_copy(
                src_ref=src,
                dst_ref=dst.at[at],
                send_sem=proj_sem.at[index],
                recv_sem=proj_sem.at[index + 1],
                device_id={"table": to(s)},
                device_id_type=MESH,
            )

        every = dst.at[pl.ds(0, n - 1)]
        both = pltpu.make_async_remote_copy(
            src_ref=every,
            dst_ref=every,
            send_sem=proj_sem.at[index],
            recv_sem=proj_sem.at[index + 1],
            device_id={"table": t},
            device_id_type=MESH,
        )
        return (lambda: each(n, lambda s: copy(s).start())), both

    z_start, z_every = along(proj_sum, proj_z, tz, 4, lambda s: ty * 4 + (tz + s) % 4, 2)
    y_start, y_every = along(proj_y, proj_all, ty, 8, lambda s: ((ty + s) % 8) * 4 + tz, 4)

    def local(src, dst, index):
        return pltpu.make_async_copy(src, dst, in_sem.at[index])

    barrier = pltpu.get_barrier_semaphore()
    near = (fs(1, 0, 0), fs(2, 0, 0), fs(0, 1, 0), fs(0, 3, 0), fs(0, 0, 1))

    def greet(axis, to):
        pl.semaphore_signal(barrier, inc=1, device_id={axis: to}, device_id_type=MESH)

    greet("fsdp", near[0])
    greet("fsdp", near[1])
    for dy in (4, 3, 5, 2, 6, 1, 7):
        greet("table", ((ty + dy) % 8) * 4 + tz)
    for dz in (2, 3, 1):
        greet("table", ty * 4 + (tz + dz) % 4)
    for other in near[2:]:
        greet("fsdp", other)

    inputs = [
        local(w_hbm, w_ref, 0),
        local(lk_hbm, lk_ref, 1),
        local(as_row_hbm, as_row_ref, 2),
        local(cot_hbm, cot_ref, 3),
        local(block_hbm, block_ref, 4),
    ]
    for copy in inputs:
        copy.start()

    inputs[0].wait()
    padded[0:SHARD_ROWS] = w_ref[...]
    padded[SHARD_ROWS:PIECE_ROWS] = jnp.zeros((PIECE_ROWS - SHARD_ROWS, 128), bf16)
    inputs[1].wait()
    pack[:, :, 0:D] = lk_ref[:, 0]
    pack[:, :, D : 2 * D] = lk_ref[:, 1]
    pl.semaphore_wait(barrier, 10 + len(near))
    for dz in (2, 3, 1):
        pl.semaphore_signal(
            line_ready, inc=1, device_id={"table": ty * 4 + (tz + dz) % 4}, device_id_type=MESH
        )

    def piece(src, shard, part, index, to):
        at = pl.ds(part * HALF_ROWS, HALF_ROWS)
        return pltpu.make_async_remote_copy(
            src_ref=src.at[at],
            dst_ref=all_ref.at[shard, at],
            send_sem=w_send.at[index],
            recv_sem=w_recv.at[index],
            device_id={"fsdp": to},
            device_id_type=MESH,
        )

    sent = []
    locals_started = []

    def drain():
        for copy in locals_started:
            copy.wait()
        for copy in sent:
            copy.wait_send()
        for exchange in started:
            if exchange not in received:
                exchange.wait()
        for exchange in started:
            exchange.wait_send()

    def send(*args):
        copy = piece(*args)
        copy.start()
        sent.append(copy)

    def forward(shard, part, index, to):
        send(all_ref.at[shard], shard, part, index + part, to)

    def arrived(shard, part, index):
        piece(all_ref.at[shard], shard, part, index + part, f).wait_recv()

    up_z, down_z, right, left, sibling = near
    for part in range(2):
        send(padded, f, part, part, up_z)
        send(padded, f, part, 2 + part, down_z)
    for part in range(2):
        send(padded, f, part, 4 + part, right)
        send(padded, f, part, 10 + part, left)
        send(padded, f, part, 22 + part, sibling)
    started.append(row_in)
    for dz in range(1, 4):
        row_in.copy_to(ty * 4 + (tz + dz) % 4).start()
    each(8, lambda s: row_in.copy_to(((ty + s) % 8) * 4 + tz).start())
    all_ref[pl.ds(f, 1)] = padded[...][None]
    arr[pl.ds(t, 1)] = pack[pl.ds(t, 1)]

    for copy in inputs[2:]:
        copy.wait()
    by_model[...] = one_hot(as_row_ref[...] == iota((NF, NF), 0))
    lane = iota((256, 256), 1)
    here = jnp.where(lane < NLC, lane + NFM, 2 * ((lane - NLC) % 8) + (lane - NLC) // 8)
    order[...] = one_hot(here == iota((256, 256), 0))
    upstream[...] = nn(cot_ref[...], order[...])

    pl.semaphore_wait(line_ready, 3)
    for dz in range(1, 4):
        each(8, lambda s: row_in.copy_to(((ty + s) % 8) * 4 + (tz + dz) % 4).start())

    def from_z(part):
        for index, dz in ((0, 2), (2, 1)):
            shard = fs(dz, 0, 0)
            arrived(shard, part, index)
            forward(shard, part, 4 + 2 * dz, right)
            forward(shard, part, 10 + 2 * dz, left)
            forward(shard, part, 22 + 8 * dz, sibling)

    def turn(dz, part):
        shard = fs(dz, 3, 0)
        arrived(shard, part, 4 + 2 * dz)
        if part == 0:
            forward(shard, part, 16 + 2 * dz, right)
        forward(shard, part, 22 + 8 * dz + 6, sibling)
        shard = fs(dz, 1, 0)
        arrived(shard, part, 10 + 2 * dz)
        if part == 1:
            forward(shard, part, 16 + 2 * dz, left)
        forward(shard, part, 22 + 8 * dz + 2, sibling)

    def opposite(dz, part):
        shard = fs(dz, 2, 0)
        arrived(shard, part, 16 + 2 * dz)
        forward(shard, part, 22 + 8 * dz + 4, sibling)

    def assemble(dz, dx):
        column = ((z + dz) % 3) * 4 + (xx + dx) % 4
        both = [all_ref[2 * column + core].astype(f32)[:SHARD_ROWS] for core in range(2)]
        at = pl.multiple_of(2 * SHARD_ROWS * column, 8)
        nat[pl.ds(at, 2 * SHARD_ROWS), :] = jnp.concatenate(both, axis=0)

    def column(dz, dx):
        for part in range(2):
            arrived(fs(dz, dx, 1), part, 22 + 8 * dz + 2 * dx)
        assemble(dz, dx)

    for part in range(2):
        turn(0, part)
    column(0, 0)

    p_lane = iota((NF, NF), 1)
    to_owner[...] = one_hot(iota((NF, NF), 0) == (p_lane % 16) * 32 + p_lane // 16)
    at, source = iota((NT * 8, NF), 0), iota((NT * 8, NF), 1)
    owner_sum[...] = one_hot((at // 8 == source // 16) & (at % 8 == (source // 8) % 2))
    at, source = iota((NT * 8, 48), 0), iota((NT * 8, 48), 1)
    mine_here = (24 * (at % 8 - 2) + 8 * ((at // 8) % 3) + at // 24 == source) & (at % 8 >= 2) & (at % 8 < 4) & (at < 192)
    mixed_place[...] = one_hot(mine_here)
    at = iota((256, 256), 0)
    wanted = 32 * (at % 8) + at // 8
    linear_place[...] = one_hot(jnp.where(wanted < NLC, wanted, -1) == iota((256, 256), 1))
    block_place[...] = one_hot(iota((NFS * SLOTS, 384), 0) == block_ref[pl.ds(t, 1), :])

    from_z(0)
    for part in range(2):
        opposite(0, part)
    from_z(1)
    for dx in (3, 1, 2):
        column(0, dx)
    for part in range(2):
        for dz in (2, 1):
            turn(dz, part)
    for dz in (2, 1):
        column(dz, 0)

    row_in.wait()
    x = nn(by_model[...], arr[...].reshape(NF, 2 * D)).astype(bf16)
    eye = one_hot(iota((2 * D, 2 * D), 0) == iota((2 * D, 2 * D), 1))
    xt = nt(eye, x).astype(bf16)

    for part in range(2):
        for dz in (2, 1):
            opposite(dz, part)
    for dz in (2, 1):
        for dx in (3, 1):
            column(dz, dx)
    for dz in (2, 1):
        column(dz, 2)

    lin = jnp.concatenate([nat[pl.ds(q, NLC, stride=4), :] for q in range(4)], axis=1)
    lin = jnp.concatenate([lin, jnp.zeros((16, NF), f32)], axis=0).astype(bf16)
    def normalise(v, c):
        v, c = v.reshape(2, D, -1), c.reshape(2, D, -1)
        mean = lambda u: jnp.mean(u, axis=1, keepdims=True)
        centred_v = v - mean(v)
        scale = lax.rsqrt(mean(centred_v * centred_v) + 1e-05)
        n = centred_v * scale
        d = scale * (c - mean(c) - n * mean(c * n))
        return n.reshape(2 * D, -1).astype(bf16), d.reshape(2 * D, -1).astype(bf16)

    linear_out, d_linear = normalise(nt(xt, lin), upstream[...])
    d_lin = nt(linear_place[...], d_linear).astype(bf16)

    def by_owner_rows(v):
        return jnp.concatenate([lanes(v, 0, 128).reshape(NT, 8, 128), lanes(v, 128, 128).reshape(NT, 8, 128)], axis=1)

    halves = [by_owner_rows(nt(d_lin, rows(x, 256 * core, 256))) for core in range(2)]
    pair_out[...] = jnp.where(c == 0, halves[1], halves[0]).astype(bf16)
    kept[...] = jnp.where(c == 0, halves[0], halves[1])
    swap = pltpu.make_async_remote_copy(
        src_ref=pair_out,
        dst_ref=pair_in,
        send_sem=own_sem.at[0],
        recv_sem=own_sem.at[1],
        device_id={"fsdp": sibling},
        device_id_type=MESH,
    )
    swap.start()
    sent.append(swap)

    for chunk in range(24):
        wout[:, 128 * chunk : 128 * chunk + 128] = nat[pl.ds(OUT_ROW + chunk, HID, stride=24), :].astype(bf16)
    proj_rows = nat[PROJ_ROW : PROJ_ROW + 32, :].astype(bf16)
    up = nat[UP_ROW : UP_ROW + NF * RANK, :].astype(bf16)

    swap.wait_recv()
    lin_msg[...] = (kept[...] + pair_in[...].astype(f32)).astype(bf16)
    lin_out.start()

    r8 = one_hot(iota((8, 128), 1) % 8 == iota((8, 128), 0))
    flat_mask = iota((NF, 128), 1) // 8 == iota((NF, 128), 0) % 16
    picked = nn(one_hot(iota((NF, 32), 1) == iota((NF, 32), 0) // 16), proj_rows)
    picked = jnp.where(flat_mask, picked, 0.0).astype(bf16)
    proj_t = nt(r8, picked).astype(bf16)

    half = iota((16, 2 * D), 1) // D == iota((16, 2 * D), 0) // 8
    comp = nn(proj_t, x)
    comp = jnp.concatenate([comp, comp], axis=0)
    comp = jnp.where(half, comp, 0.0).astype(bf16)
    pair = nt(comp, x)

    def per_sample(v):
        total = jnp.sum(v.reshape(2, 8, NF), axis=(1, 2), keepdims=True) * (1.0 / (NF * RANK))
        return jnp.broadcast_to(total, (2, 8, NF)).reshape(16, NF)

    centred = pair - per_sample(pair)
    pair_scale = lax.rsqrt(per_sample(centred * centred) + 1e-05)
    normed_full = centred * pair_scale
    normed = normed_full.astype(bf16)
    row_mod = iota((16, 128), 0) % 8
    wide = jnp.concatenate(spread(normed.astype(f32), row_mod), axis=1).astype(bf16)
    preact = jnp.sum(nn(wide, up).reshape(2, 8, HID), axis=1)
    logistic = 1.0 / (1.0 + jnp.exp(-preact))
    hidden = (preact / (1.0 + jnp.exp(-preact))).astype(bf16)
    mixed = nn(hidden, wout[...])

    def by_pairs(b):
        return jnp.concatenate([lanes(mixed[b : b + 1], 384 * e, 384) for e in range(8)], axis=0)

    m0, m1 = by_pairs(0), by_pairs(1)
    mix = jnp.concatenate(
        [
            jnp.concatenate([lanes(m0, 0, D), lanes(m1, 0, D)], axis=1),
            jnp.concatenate([lanes(m0, D, D), lanes(m1, D, D)], axis=1),
        ],
        axis=0,
    )
    mix = jnp.concatenate([jnp.zeros((112, 2 * D), f32), mix], axis=0).T
    mixed_out, d_mix = normalise(mix, lanes(upstream[...], 128, 128))
    late = iota((2 * D, 128), 1) >= 112

    def join(a, b):
        high = jnp.where(late, b.astype(f32), lanes(a, 128, 128).astype(f32)).astype(bf16)
        return jnp.concatenate([lanes(a, 0, 128), high], axis=1)

    d_low = join(d_linear, d_mix)
    d_mix = nt(one_hot(iota((16, 128), 1) == iota((16, 128), 0) + 112), d_mix)
    d_pairs = [
        jnp.concatenate([lanes(d_mix[0:8], b * D, D), lanes(d_mix[8:16], b * D, D)], axis=1) for b in range(2)
    ]
    d_mixed = jnp.concatenate(
        [jnp.concatenate([d_pairs[b][e : e + 1] for e in range(8)], axis=1) for b in range(2)], axis=0
    )
    d_hidden = nt(d_mixed.astype(bf16), wout[...])
    d_preact = (d_hidden * logistic * (1.0 + preact * (1.0 - logistic))).astype(bf16)


    by_owner = jnp.concatenate(spread(nn(normed, to_owner[...]), row_mod), axis=0).astype(bf16)
    first = nn(owner_sum[...], by_owner)
    zero = jnp.zeros((2, HID), f32)
    tile = jnp.concatenate([zero, hidden.astype(f32), zero, zero], axis=0)
    first = first.reshape(NT, 8, HID) + tile[None]
    chunks = jnp.concatenate([lanes(d_pairs[b], 128 * q, 128) for b in range(2) for q in range(3)], axis=0)
    second = nn(mixed_place[...], chunks.astype(bf16))
    tile = jnp.concatenate([d_preact.astype(f32), zero, zero, zero], axis=0)
    second = second.reshape(NT, 8, HID) + tile[None]
    fac_msg[...] = jnp.concatenate([first, second], axis=1).astype(bf16)
    fac_out.start()

    copies = jnp.concatenate(
        [jnp.broadcast_to(d_preact.astype(f32)[b : b + 1], (8, HID)) for b in range(2)], axis=0
    ).astype(bf16)
    d_normed = gather_back(nt(copies, up), row_mod)
    d_pair = pair_scale * (d_normed - per_sample(d_normed) - normed_full * per_sample(d_normed * normed_full))
    d_pair = d_pair.astype(bf16)

    d_comp = jnp.where(half, nn(d_pair, x), 0.0)
    d_comp = (d_comp[0:8] + d_comp[8:16]).astype(bf16)

    grad_proj = nt(d_comp, x).astype(bf16)
    flat = jnp.where(flat_mask, tn(grad_proj, r8), 0.0).astype(bf16)
    proj_mine[...] = nn(one_hot(iota((32, NF), 1) // 16 == iota((32, NF), 0)), flat).astype(bf16)
    proj_out = pltpu.make_async_remote_copy(
        src_ref=proj_mine,
        dst_ref=proj_parts.at[f],
        send_sem=proj_sem.at[0],
        recv_sem=proj_sem.at[1],
        device_id={"fsdp": PROJ_F},
        device_id_type=MESH,
    )

    @pl.when(f != PROJ_F)
    def _():
        proj_out.start()
        proj_all[...] = jnp.zeros_like(proj_all)

    left_side = jnp.concatenate([comp, d_comp], axis=0)
    right_side = jnp.concatenate([d_pair, proj_t], axis=0)
    d_input = (tn(left_side, right_side) + nn(d_low, lin)).astype(bf16)
    back[...] = lax.dot_general(
        by_model[...], d_input, (((0,), (1,)), ((), ())), preferred_element_type=f32
    ).astype(bf16).reshape(NT, 16, 2 * D)

    got_lin[pl.ds(t, 1)] = lin_msg[pl.ds(t, 1)]
    got_fac[pl.ds(t, 1)] = fac_msg[pl.ds(t, 1)]
    rec_ref[pl.ds(t, 1)] = back[pl.ds(t, 1)]
    out_ref[...] = nt(join(linear_out, mixed_out), order[...]).astype(bf16)
    result = local(out_ref, out_hbm, 5)
    result.start()
    locals_started.append(result)

    lin_out.wait()
    linear = jnp.sum(got_lin[...].astype(f32), axis=0)
    fac_out.wait()
    factors = got_fac[...].astype(f32)
    first = factors[:, 0:8].reshape(NT * 8, 128)
    second = factors[:, 8:16].reshape(NT * 8, 128).astype(bf16)
    at = iota((NT * 8, 128), 0) % 8
    left_side = jnp.concatenate([jnp.where(at < 2, first, 0.0), jnp.where((at == 2) | (at == 3), first, 0.0)], axis=1)
    products = tn(left_side.astype(bf16), second)
    sums = jnp.concatenate(
        [
            products,
            jnp.where(c == 0, linear, 0.0),
            jnp.where(c == 1, linear, 0.0),
            jnp.zeros((96, 128), f32),
        ],
        axis=0,
    ).astype(bf16)
    blocks[...] = nn(block_place[...], sums).astype(bf16).reshape(NFS, SLOTS, 128)

    to_fsdp.start()

    @pl.when(f == PROJ_F)
    def _():
        others = proj_parts.at[pl.ds(0, NFS - 1)]
        pltpu.make_async_remote_copy(
            src_ref=others,
            dst_ref=others,
            send_sem=proj_sem.at[0],
            recv_sem=proj_sem.at[1],
            device_id={"fsdp": f},
            device_id_type=MESH,
        ).wait_recv()
        proj_parts[pl.ds(f, 1)] = proj_mine[...][None]
        proj_sum[...] = jnp.sum(proj_parts[...].astype(f32), axis=0).astype(bf16)
        z_start()
        proj_z[pl.ds(tz, 1)] = proj_sum[...][None]

    row_out.start()

    @pl.when(f == PROJ_F)
    def _():
        z_every.wait_recv()
        proj_y[...] = jnp.sum(proj_z[...].astype(f32), axis=0).astype(bf16)
        y_start()
        proj_all[pl.ds(ty, 1)] = proj_y[...][None]

    parts[pl.ds(f, 1)] = blocks[pl.ds(f, 1)]
    to_fsdp.wait()
    mine[...] = jnp.sum(parts[...].astype(f32), axis=0).astype(bf16)

    all_out.start()
    whole_ref[pl.ds(t, 1)] = mine[...][None]
    all_out.wait()
    row_out.wait()

    @pl.when(f == PROJ_F)
    def _():
        y_every.wait_recv()
        z_every.wait_send()
        y_every.wait_send()

    @pl.when(f != PROJ_F)
    def _():
        proj_out.wait_send()

    drain()


def finish_kernel(out_ref, rec_ref, whole_ref, proj_ref, row_ref, layer_ref, emb_ref, grad_ref):
    f = lax.axis_index("fsdp")
    layer_ref[...] = out_ref[...]
    emb_ref[:, 0] = rec_ref[:, :, 0:D]
    emb_ref[:, 1] = rec_ref[:, :, D : 2 * D]
    final = one_hot(iota((SHARD_ROWS, NT * SLOTS), 0) == row_ref[pl.ds(f, 1), :])
    grad_ref[...] = nn(final, whole_ref[...].reshape(NT * SLOTS, 128)) * (1.0 / SAMPLES)

    @pl.when(f == PROJ_F)
    def _():
        at = pl.ds(PROJ_ROW - PROJ_F * SHARD_ROWS, 32)
        grad_ref[at, :] = jnp.sum(proj_ref[...].astype(f32), axis=0) * (1.0 / SAMPLES)


VMEM = pl.BlockSpec(memory_space=pltpu.VMEM)
IN_HBM = pl.BlockSpec(memory_space=pltpu.HBM)
LIMIT = 40 * 1024 * 1024


def shape(dtype, *size):
    return jax.ShapeDtypeStruct(size, dtype)


def whole(looked, shard, as_row, cotangent):
    return pl.pallas_call(
        whole_kernel,
        out_shape=(
            shape(bf16, 2 * D, 256),
            shape(bf16, NT, 16, 2 * D),
            shape(bf16, NT, SLOTS, 128),
            shape(bf16, 8, 32, 128),
        ),
        in_specs=[IN_HBM] * 5,
        out_specs=(IN_HBM, VMEM, VMEM, VMEM),
        scratch_shapes=[
            pltpu.VMEM((NT, 2, 16, D), bf16),
            pltpu.VMEM((SHARD_ROWS, 128), bf16),
            pltpu.VMEM((1, NF), jnp.int32),
            pltpu.VMEM((2 * D, 256), bf16),
            pltpu.VMEM((NT, 384), jnp.int32),
            pltpu.VMEM((2 * D, 256), bf16),
            pltpu.VMEM((NT, 16, 2 * D), bf16),
            pltpu.VMEM((PIECE_ROWS, 128), bf16),
            pltpu.VMEM((NT, 16, 2 * D), bf16),
            pltpu.VMEM((NFS, PIECE_ROWS, 128), bf16),
            pltpu.VMEM((TOTAL_ROWS, 128), f32),
            pltpu.VMEM((HID, NFM * D), bf16),
            pltpu.VMEM((NF, NF), bf16),
            pltpu.VMEM((256, 256), bf16),
            pltpu.VMEM((2 * D, 256), f32),
            pltpu.VMEM((NF, NF), bf16),
            pltpu.VMEM((NT * 8, NF), bf16),
            pltpu.VMEM((NT * 8, 48), bf16),
            pltpu.VMEM((256, 256), bf16),
            pltpu.VMEM((NFS * SLOTS, 384), bf16),
            pltpu.VMEM((NT, 16, 128), bf16),
            pltpu.VMEM((NT, 16, 128), bf16),
            pltpu.VMEM((NT, 16, 128), f32),
            pltpu.VMEM((NT, 16, 128), bf16),
            pltpu.VMEM((NT, 16, 128), bf16),
            pltpu.VMEM((NT, 16, 2 * D), bf16),
            pltpu.VMEM((NT, 16, 128), bf16),
            pltpu.VMEM((NT, 16, 128), bf16),
            pltpu.VMEM((NFS, SLOTS, 128), bf16),
            pltpu.VMEM((NFS, SLOTS, 128), bf16),
            pltpu.VMEM((SLOTS, 128), bf16),
            pltpu.VMEM((32, 128), bf16),
            pltpu.VMEM((NFS, 32, 128), bf16),
            pltpu.VMEM((32, 128), bf16),
            pltpu.VMEM((4, 32, 128), bf16),
            pltpu.VMEM((32, 128), bf16),
            pltpu.SemaphoreType.REGULAR,
            pltpu.SemaphoreType.DMA((2,)),
            pltpu.SemaphoreType.DMA((6,)),
            pltpu.SemaphoreType.DMA((6,)),
            pltpu.SemaphoreType.DMA((46,)),
            pltpu.SemaphoreType.DMA((46,)),
            pltpu.SemaphoreType.DMA((6,)),
            pltpu.SemaphoreType.DMA((6,)),
        ],
        compiler_params=pltpu.CompilerParams(collective_id=0, has_side_effects=True, vmem_limit_bytes=LIMIT),
    )(*[pltpu.with_memory_space_constraint(v, pltpu.HBM) for v in (looked, shard, as_row, cotangent, jnp.asarray(TO_BLOCK))])


def finish(out, rec, gathered, proj):
    return pl.pallas_call(
        finish_kernel,
        out_shape=(shape(bf16, 2 * D, 256), shape(bf16, NT, 2, 16, D), shape(f32, SHARD_ROWS, 128)),
        in_specs=[VMEM] * 5,
        out_specs=(VMEM,) * 3,
        compiler_params=pltpu.CompilerParams(vmem_limit_bytes=12 * 1024 * 1024),
    )(out, rec, gathered, proj, jnp.asarray(TO_ROW))


def shards(looked_up, assignment, flat_weights, cotangent):
    out, rec, gathered, proj = whole(
        looked_up.reshape(NT, 2, 16, D),
        flat_weights.reshape(SHARD_ROWS, 128),
        assignment.reshape(1, NF),
        cotangent.transpose(0, 2, 1).reshape(2 * D, 256),
    )
    layer_out, emb, grad = finish(out, rec, gathered, proj)
    return layer_out.reshape(2, D, 256).transpose(0, 2, 1), emb.reshape(2 * NT, 16, D), grad.reshape(SHARD_ROWS * 128)


def solution(mesh):
    return jax.shard_map(
        shards,
        mesh=mesh,
        in_specs=(P("fsdp", "table", None), P(), P("fsdp"), P(("fsdp", "table"), None, None)),
        out_specs=(P(("fsdp", "table"), None, None), P("fsdp", "table", None), P("fsdp")),
        check_vma=False,
    )
```
